256 devices in a mesh: blk: 32 (over z, y_hi, core), head: 8 (over x, y_lo).
Axes of the slice: x: 4, y: 4 (y_hi: 2, y_lo: 2; y = y_hi * 2 + y_lo), z: 8, core: 2. Of those that a mesh axis runs over, the one named last changes fastest.
Arguments:
- frames: bfloat16 [32768, 2048], P(('blk', 'head')), may hold values from -20.4 to 20.4
- qkv_weight: bfloat16 [2048, 6144], P(None, 'head'), may hold values from -0.125 to 0.125
- out_weight: bfloat16 [2048, 2048], P('head'), may hold values from -0.125 to 0.125
- recording: int32 [32768], P(('blk', 'head')), may hold values from 0 to 63, never falling along the last dimension, each value on 1 to 1024 neighbouring positions
Outputs:
- encoded: bfloat16 [32768, 2048], P(('blk', 'head'))
The draws below stay inside these ranges and needn't reach their ends.
Inputs may be any that keep to these rules, and one draw needn't show every extreme that they name: Recording ids never fall along the frames; each recording holds 1 to 1024 frames, and one holds exactly 1024.
All inputs are finite; a program needn't handle non-finite values.
Results may differ from the reference program's by a relative error of at most 0.019.
The reference program's roundings to bfloat16 on the way count: a program that leaves them out, or rounds other values in their place, can miss the bound.
Values may be sent and summed in bfloat16 or wider, within the bound.
A program may use at most 64 MiB of HBM per device.

```python
import math
import jax
import jax.numpy as jnp
import numpy as np
from jax import lax

D = 2048
HEADS = 16
HEAD_DIM = 128
FRAMES_DEV = 128
REACH = 1
TOKENS = 32768
SPAN = 1024
RECORDINGS = 64
N_HEAD = 8


def draw_frames(key, part):
    key = jax.random.fold_in(key, 11)
    row_key, value_key = jax.random.split(key)
    scales = jnp.exp(jax.random.uniform(row_key, (TOKENS, 1), jnp.float32, 0.0, math.log(3.0)))
    values = jax.random.truncated_normal(value_key, -4.0, 4.0, (TOKENS, D), jnp.float32)
    return (scales * values).astype(jnp.bfloat16)


def levels(own_key, dims, cuts, smallest, high):
    factor_of, own = 1.0, jax.random.fold_in(own_key, 6)
    for dim, parts in cuts:
        heights = jnp.exp(jax.random.uniform(jax.random.fold_in(own, dim), (parts,), jnp.float32, smallest / len(cuts), high / len(cuts)))
        factor_of = factor_of * jnp.repeat(heights, dims[dim] // parts).reshape([-1 if axis == dim else 1 for axis in range(len(dims))])
    return factor_of


def split_up(amount, total, reach, lean):
    weights = [(1 << 20) // math.isqrt(standing ** lean) + 1 for standing in range(2, amount + 1)]
    rest, holding = total - reach - (amount - 1), [1] * (amount - 1)
    while rest > 0:
        candidates = [i for i in range(amount - 1) if holding[i] < reach]
        mass, budget = sum([weights[i] for i in candidates]), rest
        for i in candidates:
            more = min(reach - holding[i], max(1, budget * weights[i] // mass), rest)
            holding[i] = holding[i] + more
            rest = rest - more
    return np.array([reach] + holding)


def uneven_parts(stream_key, number_of, total, limit, skew):
    if number_of == 2:
        one = jax.random.randint(stream_key, (), max(1, total - limit), min(limit, total - 1) + 1)
        return jnp.stack([one, total - one])
    sizes = jnp.asarray(split_up(number_of, total, limit, skew), jnp.int32)
    twos = (number_of - 1) // 2
    donor, sink = sizes[1:1 + 2 * twos:2], sizes[2:2 + 2 * twos:2]
    room = jnp.minimum(donor - 1, limit - sink)
    passed = jax.random.randint(jax.random.fold_in(stream_key, 1), (twos,), 0, 1 << 20) % (room + 1)
    sizes = sizes.at[1:1 + 2 * twos:2].set(donor - passed).at[2:2 + 2 * twos:2].set(sink + passed)
    return sizes[jax.random.permutation(jax.random.fold_in(stream_key, 2), number_of)]


def scatter_about(own_key, dims, width, limit, cuts=(), kind=jnp.bfloat16):
    result = jax.random.normal(own_key, dims, jnp.float32) * width
    if len(cuts) > 0:
        result = levels(own_key, dims, cuts, -0.22, 0.18) * result
    return jnp.clip(result, min=-limit, max=limit).astype(kind)


def setup_inputs(seed: int = 0) -> dict:
    seeds = jax.random.split(jax.random.key(seed), 5)
    frames = draw_frames(jax.random.fold_in(seeds[4], 71), 0)
    qkv_weight = scatter_about(seeds[1], (D, 3 * D), D ** -0.5, 0.125, ((1, 8),))
    out_weight = scatter_about(seeds[2], (D, D), D ** -0.5, 0.125, ((0, 8),))
    recording = jnp.searchsorted(jnp.cumsum(uneven_parts(seeds[3], RECORDINGS, TOKENS, SPAN, 2)), jnp.arange(TOKENS), side="right").astype(jnp.int32)
    return {"frames": frames, "qkv_weight": qkv_weight, "out_weight": out_weight, "recording": recording}


def reference(frames, qkv_weight, out_weight, recording):
    group = FRAMES_DEV * N_HEAD
    count = TOKENS // group
    margin = REACH * group
    qkv = jnp.dot(frames, qkv_weight, preferred_element_type=jnp.float32).astype(jnp.bfloat16)
    qkv = qkv.reshape(TOKENS, HEADS, 3, HEAD_DIM)
    query = qkv[:, :, 0, :]
    keys = qkv[:, :, 1, :]
    values = qkv[:, :, 2, :]

    def padded(array):
        edge = jnp.zeros((margin,) + array.shape[1:], array.dtype)
        return jnp.concatenate([edge, array, edge], axis=0)

    key_pad = padded(keys)
    value_pad = padded(values)
    edge_ids = jnp.full((margin,), -1, jnp.int32)
    id_pad = jnp.concatenate([edge_ids, recording.astype(jnp.int32), edge_ids], axis=0)
    window = 2 * margin + group

    def one_block(index):
        start = (index * group).astype(jnp.int32)
        local_query = lax.dynamic_slice_in_dim(query, start, group, 0).astype(jnp.float32)
        query_ids = lax.dynamic_slice_in_dim(recording.astype(jnp.int32), start, group, 0)
        local_keys = lax.dynamic_slice_in_dim(key_pad, start, window, 0).astype(jnp.float32)
        local_values = lax.dynamic_slice_in_dim(value_pad, start, window, 0).astype(jnp.float32)
        key_ids = lax.dynamic_slice_in_dim(id_pad, start, window, 0)
        scores = jnp.einsum("qhd,khd->hqk", local_query, local_keys) * (HEAD_DIM ** -0.5)
        mask = query_ids[:, None] == key_ids[None, :]
        scores = jnp.where(mask[None, :, :], scores, -jnp.inf)
        top = jnp.max(scores, axis=2, keepdims=True)
        weights = jnp.exp(scores - top)
        totals = jnp.sum(weights, axis=2)
        rounded = lax.optimization_barrier(weights.astype(jnp.bfloat16)).astype(jnp.float32)
        mixed = jnp.einsum("hqk,khd->qhd", rounded, local_values)
        mixed = mixed / jnp.transpose(totals)[:, :, None]
        return mixed.astype(jnp.bfloat16).reshape(group, D)

    attended = lax.map(one_block, jnp.arange(count, dtype=jnp.int32)).reshape(TOKENS, D)
    return jnp.dot(attended, out_weight, preferred_element_type=jnp.float32).astype(jnp.bfloat16)
```

```python
import functools

import jax
import jax.numpy as jnp
from jax import lax
from jax.experimental import pallas as pl
from jax.experimental.pallas import tpu as pltpu
from jax.sharding import PartitionSpec as P

HEAD_DIM = 128
MESH = pl.DeviceIdType.MESH
NX, NZ, NB = 4, 8, 32
BF = jnp.bfloat16
F32 = jnp.float32
NEG = -jnp.inf


def mod(a, n):
    return lax.rem(a + 2 * n, n)


def kernel(
    frames, qw_in, ow, ids, out,
    F, QW, W, Q, KV, H, RL, IDS, HID, RID, QID, ATS, ATR, ACC, M, L, A,
    loc, ag_s, ag_r, id_s, id_r, hid_s, hid_r, sib_s, sib_r, off_s, off_r, rel_s, rel_r,
    wp_s, wp_r, wu_s, wu_r, wd_s, wd_r, ws_s, ws_r, at_s, at_r,
):
    blk = lax.axis_index("blk")
    head = lax.axis_index("head")
    z = blk // 4
    yh = lax.rem(blk, 4) // 2
    c = lax.rem(blk, 2)
    x = head // 2
    yl = lax.rem(head, 2)

    def block(dx, f):
        return mod(x + dx, NX) * 2 + lax.rem(yl + f, 2)

    def peer(dx, f):
        return (blk, block(dx, f))

    right, left, across = peer(1, 0), peer(-1, 0), peer(0, 1)
    sibling = (blk + 1 - 2 * c, head)
    above = (mod(blk + 4, NB), head)
    below = (mod(blk - 4, NB), head)
    owner_blk = z * 4 + (1 - yh) * 2 + c
    owner_head = x * 2 + 1 - yl
    relay = (owner_blk, owner_head)
    relay_to = (mod(owner_blk + 2 * c - 1, NB), owner_head)
    far = mod(blk + 2 * c - 1, NB)
    relay_from = ((far // 4) * 4 + (1 - lax.rem(far, 4) // 2) * 2 + lax.rem(far, 2), owner_head)
    base_off = 8 * (1 - c)
    base_sib = 8 * c

    def remote(src, dst, ss, rs, dev):
        return pltpu.make_async_remote_copy(
            src_ref=src, dst_ref=dst, send_sem=ss, recv_sem=rs, device_id=dev, device_id_type=MESH
        )

    load_qw = pltpu.make_async_copy(qw_in, QW, loc.at[0])
    load_own = pltpu.make_async_copy(frames, F.at[head], loc.at[1])
    load_w = pltpu.make_async_copy(ow, W.at[0], loc.at[2])
    load_own.start()
    load_qw.start()
    load_w.start()
    rels = [(dx, f) for dx in range(NX) for f in range(2)]
    partners = [peer(dx, f) for dx, f in rels[1:]]
    partners += [sibling, above, below, relay, relay_to, relay_from]
    barrier = pltpu.get_barrier_semaphore()
    for p in partners:
        pl.semaphore_signal(barrier, inc=1, device_id=p, device_id_type=MESH)
    pl.semaphore_wait(barrier, len(partners))

    piece = [None]
    for k in range(1, 8):
        dx, f = rels[k]
        back = ((-dx) % NX) * 2 + f
        piece.append(remote(ow.at[z, c], W.at[back, z, c], wp_s.at[k], wp_r.at[back], peer(dx, f)))
    for k in (1, 2, 6, 3, 7, 4, 5):
        piece[k].start()

    def fr(dx, f, half=None):
        ref = F.at[block(dx, f)]
        if half is None:
            return ref
        return ref.at[pl.ds(64 * half, 64)]

    def gather_copy(i, src, dst, dev):
        return remote(src, dst, ag_s.at[i], ag_r.at[i], dev)

    send = [
        gather_copy(0, frames, fr(0, 0), right),
        gather_copy(1, frames, fr(0, 0), left),
        gather_copy(2, frames, fr(0, 0), across),
        gather_copy(3, fr(-1, 0, 0), fr(-1, 0, 0), right),
        gather_copy(4, fr(1, 0, 1), fr(1, 0, 1), left),
        gather_copy(5, fr(0, 1), fr(0, 1), right),
        gather_copy(6, fr(0, 1), fr(0, 1), left),
        gather_copy(7, fr(-1, 1, 0), fr(-1, 1, 0), right),
        gather_copy(8, fr(1, 1, 1), fr(1, 1, 1), left),
    ]
    recv = [
        gather_copy(0, fr(-1, 0), fr(-1, 0), right),
        gather_copy(1, fr(1, 0), fr(1, 0), right),
        gather_copy(2, fr(0, 1), fr(0, 1), right),
        gather_copy(3, fr(2, 0, 0), fr(2, 0, 0), right),
        gather_copy(4, fr(2, 0, 1), fr(2, 0, 1), right),
        gather_copy(5, fr(-1, 1), fr(-1, 1), right),
        gather_copy(6, fr(1, 1), fr(1, 1), right),
        gather_copy(7, fr(2, 1, 0), fr(2, 1, 0), right),
        gather_copy(8, fr(2, 1, 1), fr(2, 1, 1), right),
    ]
    send[0].start()
    send[1].start()
    send[2].start()

    idc = [None]
    for k in range(1, 8):
        dx, f = rels[k]
        back = ((-dx) % NX) * 2 + f
        idc.append(remote(ids, IDS.at[head], id_s.at[k], id_r.at[back], peer(dx, f)))
        idc[k].start()
    IDS[head] = ids[...]

    def kv_copies(b):
        return (
            remote(KV.at[b], H.at[base_sib + b], sib_s.at[b], sib_r.at[b], sibling),
            remote(KV.at[b], RL.at[b], off_s.at[b], off_r.at[b], relay),
        )

    def relay_copy(b):
        return remote(RL.at[b], H.at[base_off + b], rel_s.at[b], rel_r.at[b], relay_to)

    def project(b):
        r = jnp.dot(F[b], QW[...], preferred_element_type=F32).astype(BF)
        for hd in range(2):
            o = hd * 3 * HEAD_DIM
            cols = pl.ds(hd * HEAD_DIM, HEAD_DIM)
            Q[b, :, cols] = r[:, o : o + HEAD_DIM]
            KV[b, 0, :, cols] = r[:, o + HEAD_DIM : o + 2 * HEAD_DIM]
            KV[b, 1, :, cols] = r[:, o + 2 * HEAD_DIM : o + 3 * HEAD_DIM]
        to_sib, to_off = kv_copies(b)
        to_off.start()
        to_sib.start()

    def pass_on(dx, f):
        b = mod(x + dx, NX) * 2 + lax.rem(1 - yl + f, 2)
        remote(RL.at[b], RL.at[b], off_s.at[b], off_r.at[b], relay).wait_recv()
        relay_copy(b).start()

    def wz(s, up):
        return mod(z - s, NZ) if up else mod(z + s, NZ)

    def w_set(zs, part):
        return W.at[pl.ds(*part), zs, c]

    FULL, UPART, DPART = (1, 7), (1, 4), (5, 3)

    def w_send(s, up):
        zs = wz(s - 1, up)
        part = FULL if s < 4 else (UPART if up else DPART)
        ref = w_set(zs, part)
        if up:
            return remote(ref, ref, wu_s.at[s], wu_r.at[s], above)
        return remote(ref, ref, wd_s.at[s], wd_r.at[s], below)

    def w_recv(s, up):
        zs = wz(s, up)
        part = FULL if s < 4 else (UPART if up else DPART)
        ref = w_set(zs, part)
        if up:
            return remote(ref, ref, wu_s.at[s], wu_r.at[s], above)
        return remote(ref, ref, wd_s.at[s], wd_r.at[s], below)

    def w_sib(j):
        ref = w_set(mod(z + j, NZ), FULL)
        return remote(ref, ref, ws_s.at[j], ws_r.at[j], sibling)

    def w_sib_recv(j):
        ref = W.at[pl.ds(*FULL), mod(z + j, NZ), 1 - c]
        return remote(ref, ref, ws_s.at[j], ws_r.at[j], sibling)

    def w_step(s):
        w_recv(s, True).wait_recv()
        w_send(s + 1, True).start()
        w_recv(s, False).wait_recv()
        w_send(s + 1, False).start()
        w_sib(8 - s).start()
        w_sib(s).start()

    load_own.wait()
    load_qw.wait()
    project(head)

    for k in range(1, 8):
        remote(W.at[k, z, c], W.at[k, z, c], wp_s.at[k], wp_r.at[k], across).wait_recv()
    w_send(1, True).start()
    w_send(1, False).start()
    w_sib(0).start()

    for k in range(1, 8):
        dx, f = rels[k]
        row = IDS.at[block(dx, f)]
        remote(row, row, id_s.at[k], id_r.at[k], across).wait_recv()
    ids_sib = remote(IDS, HID.at[pl.ds(base_sib, 8)], hid_s.at[0], hid_r.at[0], sibling)
    ids_off = remote(IDS, RID, hid_s.at[1], hid_r.at[1], relay)
    ids_rel = remote(RID, HID.at[pl.ds(base_off, 8)], hid_s.at[2], hid_r.at[2], relay_to)
    ids_off.start()
    ids_sib.start()
    for b in range(8):
        QID[b] = jnp.transpose(jnp.broadcast_to(IDS[b], (128, 128)))

    recv[0].wait_recv()
    send[3].start()
    recv[1].wait_recv()
    send[4].start()
    recv[2].wait_recv()
    send[5].start()
    send[6].start()
    pass_on(0, 0)
    ids_off.wait_recv()
    ids_rel.start()
    project(block(0, 1))
    project(block(-1, 0))
    project(block(1, 0))
    w_step(1)
    pass_on(0, 1)
    recv[3].wait_recv()
    recv[4].wait_recv()
    project(block(2, 0))
    pass_on(-1, 0)
    pass_on(1, 0)
    pass_on(2, 0)
    recv[5].wait_recv()
    send[7].start()
    recv[6].wait_recv()
    send[8].start()
    project(block(-1, 1))
    project(block(1, 1))
    w_step(2)
    pass_on(-1, 1)
    pass_on(1, 1)
    recv[7].wait_recv()
    recv[8].wait_recv()
    project(block(2, 1))
    w_step(3)
    pass_on(2, 1)

    scale = HEAD_DIM ** (-0.5)
    dims = (((1,), (1,)), ((), ()))

    own_ids = jnp.concatenate([IDS[j] for j in range(8)], axis=1)

    def own_step(i, carry):
        qid = jnp.concatenate([QID[i]] * 8, axis=1)
        mask = qid == own_ids
        for hd in range(2):
            cols = pl.ds(hd * HEAD_DIM, HEAD_DIM)
            q = Q[i, :, cols]
            k = KV[:, 0, :, cols].reshape(1024, HEAD_DIM)
            v = KV[:, 1, :, cols].reshape(1024, HEAD_DIM)
            s = lax.dot_general(q, k, dims, preferred_element_type=F32) * scale
            s = jnp.where(mask, s, NEG)
            m = jnp.max(s, axis=1, keepdims=True)
            p = jnp.exp(s - m)
            M[i, hd] = m
            L[i, hd] = jnp.sum(p, axis=1, keepdims=True)
            A[i, hd] = jnp.dot(p.astype(BF), v, preferred_element_type=F32)
        return carry

    lax.fori_loop(0, 8, own_step, 0)

    for b in range(8):
        hs, ho = H.at[8 - base_sib + b], H.at[8 - base_off + b]
        remote(hs, hs, sib_s.at[b], sib_r.at[b], sibling).wait_recv()
        remote(ho, ho, rel_s.at[b], rel_r.at[b], sibling).wait_recv()
    hs, ho = HID.at[pl.ds(8 - base_sib, 8)], HID.at[pl.ds(8 - base_off, 8)]
    remote(hs, hs, hid_s.at[0], hid_r.at[0], sibling).wait_recv()
    remote(ho, ho, hid_s.at[2], hid_r.at[2], sibling).wait_recv()

    def halo_step(t, carry):
        d = 7 - t
        dx = d // 2
        f = lax.rem(d, 2)
        i = block(dx, f)
        kid = jnp.concatenate([HID[i + j] for j in range(9)], axis=1)
        qid = jnp.concatenate([QID[i]] * 9, axis=1)
        mask = qid == kid
        for hd in range(2):
            cols = pl.ds(hd * HEAD_DIM, HEAD_DIM)
            q = Q[i, :, cols]
            k = H[pl.ds(i, 9), 0, :, cols].reshape(9 * 128, HEAD_DIM)
            v = H[pl.ds(i, 9), 1, :, cols].reshape(9 * 128, HEAD_DIM)
            s = lax.dot_general(q, k, dims, preferred_element_type=F32) * scale
            s = jnp.where(mask, s, NEG)
            m0 = M[i, hd]
            m = jnp.maximum(m0, jnp.max(s, axis=1, keepdims=True))
            p = jnp.exp(s - m)
            decay = jnp.exp(m0 - m)
            total = L[i, hd] * decay + jnp.sum(p, axis=1, keepdims=True)
            mixed = A[i, hd] * decay + jnp.dot(p.astype(BF), v, preferred_element_type=F32)
            ATS[d, :, cols] = (mixed / total).astype(BF)
        back = mod(-dx, NX) * 2 + f

        @pl.when(d > 0)
        def _():
            remote(ATS.at[d], ATR.at[back], at_s.at[d], at_r.at[back], (blk, i)).start()

        return carry

    lax.fori_loop(0, 8, halo_step, 0)

    w_recv(4, True).wait_recv()
    w_recv(4, False).wait_recv()
    w_sib(4).start()
    load_w.wait()
    for j in range(8):
        w_sib_recv(j).wait_recv()

    def out_part(a, d):
        return jnp.dot(a, W[d].reshape(256, 2048), preferred_element_type=F32)

    ACC[...] = out_part(ATS[0], 0)

    def out_step(t, carry):
        d = 7 - t
        remote(ATR.at[d], ATR.at[d], at_s.at[d], at_r.at[d], sibling).wait_recv()
        ACC[...] += out_part(ATR[d], d)
        return carry

    lax.fori_loop(0, 7, out_step, 0)
    out[...] = ACC[...].astype(BF)

    for k in range(1, 8):
        piece[k].wait_send()
        idc[k].wait_send()
        remote(ATS.at[k], ATR.at[k], at_s.at[k], at_r.at[k], sibling).wait_send()
    for i in range(9):
        send[i].wait_send()
    for b in range(8):
        to_sib, to_off = kv_copies(b)
        to_sib.wait_send()
        to_off.wait_send()
        relay_copy(b).wait_send()
        w_sib(b).wait_send()
    ids_sib.wait_send()
    ids_off.wait_send()
    ids_rel.wait_send()
    for s in range(1, 5):
        w_send(s, True).wait_send()
        w_send(s, False).wait_send()


def shards(frames, qkv_weight, out_weight, recording):
    dma = pltpu.SemaphoreType.DMA
    any_ = pl.BlockSpec(memory_space=pl.ANY)
    vmem = pl.BlockSpec(memory_space=pltpu.VMEM)
    V = pltpu.VMEM
    return pl.pallas_call(
        kernel,
        name="encoder_block",
        out_shape=jax.ShapeDtypeStruct((128, 2048), BF),
        in_specs=[any_, any_, any_, vmem],
        out_specs=vmem,
        scratch_shapes=[
            V((8, 128, 2048), BF),
            V((2048, 768), BF),
            V((8, 8, 2, 16, 2048), BF),
            V((8, 128, 256), BF),
            V((8, 2, 128, 256), BF),
            V((16, 2, 128, 256), BF),
            V((8, 2, 128, 256), BF),
            V((8, 1, 128), jnp.int32),
            V((16, 1, 128), jnp.int32),
            V((8, 1, 128), jnp.int32),
            V((8, 128, 128), jnp.int32),
            V((8, 128, 256), BF),
            V((8, 128, 256), BF),
            V((128, 2048), F32),
            V((8, 2, 128, 1), F32),
            V((8, 2, 128, 1), F32),
            V((8, 2, 128, 128), F32),
            dma((3,)),
            dma((9,)), dma((9,)),
            dma((8,)), dma((8,)),
            dma((3,)), dma((3,)),
            dma((8,)), dma((8,)),
            dma((8,)), dma((8,)),
            dma((8,)), dma((8,)),
            dma((8,)), dma((8,)),
            dma((5,)), dma((5,)),
            dma((5,)), dma((5,)),
            dma((8,)), dma((8,)),
            dma((8,)), dma((8,)),
        ],
        compiler_params=pltpu.CompilerParams(
            collective_id=0, has_side_effects=True, vmem_limit_bytes=56 * 2**20
        ),
    )(frames, qkv_weight, out_weight.reshape(8, 2, 16, 2048), recording.reshape(1, 128))


def solution(mesh):
    in_specs = (P(("blk", "head"), None), P(None, "head"), P("head", None), P(("blk", "head")))
    out_specs = P(("blk", "head"), None)
    return jax.shard_map(shards, mesh=mesh, in_specs=in_specs, out_specs=out_specs, check_vma=False)
```

```python
import functools

import jax
import jax.numpy as jnp
from jax import lax
from jax.experimental import pallas as pl
from jax.experimental.pallas import tpu as pltpu
from jax.sharding import PartitionSpec as P

HEAD_DIM = 128
MESH = pl.DeviceIdType.MESH
NX, NZ, NB = 4, 8, 32
BF = jnp.bfloat16
F32 = jnp.float32
NEG = -jnp.inf


def mod(a, n):
    return lax.rem(a + 2 * n, n)


def kernel(
    frames, qw_in, ow, ids, out,
    F, QW, W, Q, KV, H, RL, IDS, HID, RID, QID, ATS, ATR, ACC, M, L, A,
    loc, ag_s, ag_r, id_s, id_r, hid_s, hid_r, sib_s, sib_r, off_s, off_r, rel_s, rel_r,
    wp_s, wp_r, wx_s, wx_r, wu_s, wu_r, wd_s, wd_r, ws_s, ws_r, at_s, at_r,
):
    blk = lax.axis_index("blk")
    head = lax.axis_index("head")
    z = blk // 4
    yh = lax.rem(blk, 4) // 2
    c = lax.rem(blk, 2)
    x = head // 2
    yl = lax.rem(head, 2)

    def block(dx, f):
        return mod(x + dx, NX) * 2 + lax.rem(yl + f, 2)

    def peer(dx, f):
        return (blk, block(dx, f))

    right, left, across = peer(1, 0), peer(-1, 0), peer(0, 1)
    sibling = (blk + 1 - 2 * c, head)
    above = (mod(blk + 4, NB), head)
    below = (mod(blk - 4, NB), head)
    owner_blk = z * 4 + (1 - yh) * 2 + c
    owner_head = x * 2 + 1 - yl
    relay = (owner_blk, owner_head)
    relay_to = (mod(owner_blk + 2 * c - 1, NB), owner_head)
    far = mod(blk + 2 * c - 1, NB)
    relay_from = ((far // 4) * 4 + (1 - lax.rem(far, 4) // 2) * 2 + lax.rem(far, 2), owner_head)
    base_off = 8 * (1 - c)
    base_sib = 8 * c

    def remote(src, dst, ss, rs, dev):
        return pltpu.make_async_remote_copy(
            src_ref=src, dst_ref=dst, send_sem=ss, recv_sem=rs, device_id=dev, device_id_type=MESH
        )

    load_qw = pltpu.make_async_copy(qw_in, QW, loc.at[0])
    load_own = pltpu.make_async_copy(frames, F.at[head], loc.at[1])
    load_w = pltpu.make_async_copy(ow, W.at[0], loc.at[2])
    load_own.start()
    load_qw.start()
    load_w.start()
    rels = [(dx, f) for f in range(2) for dx in range(NX)]
    partners = [peer(dx, f) for dx, f in rels[1:]]
    partners += [sibling, above, below, relay, relay_to, relay_from]
    barrier = pltpu.get_barrier_semaphore()
    for p in partners:
        pl.semaphore_signal(barrier, inc=1, device_id=p, device_id_type=MESH)
    pl.semaphore_wait(barrier, len(partners))

    idc = [None]
    for k in range(1, 8):
        dx, f = rels[k]
        back = f * NX + (-dx) % NX
        idc.append(remote(ids, IDS.at[head], id_s.at[k], id_r.at[back], peer(dx, f)))
        idc[k].start()
    IDS[head] = ids[...]

    mine = pl.ds(pl.multiple_of(yh * 1024, 1024), 1024)
    other = pl.ds(pl.multiple_of((1 - yh) * 1024, 1024), 1024)
    piece = [None]
    for k in range(1, 8):
        dx, f = rels[k]
        back = f * NX + (-dx) % NX
        piece.append(
            remote(ow.at[z, c, :, mine], W.at[back, z, c, :, mine], wp_s.at[k], wp_r.at[back], peer(dx, f))
        )
        piece[k].start()

    def fr(dx, f, half):
        return F.at[block(dx, f), pl.ds(64 * half, 64)]

    def gather_copy(i, src, dst, dev):
        return remote(src, dst, ag_s.at[i], ag_r.at[i], dev)

    plan = {
        "A0": ((0, 0, 0), right, (-1, 0, 0)),
        "B1": ((0, 0, 1), left, (1, 0, 1)),
        "C0": ((0, 0, 0), across, (0, 1, 0)),
        "A1": ((0, 0, 1), right, (-1, 0, 1)),
        "B0": ((0, 0, 0), left, (1, 0, 0)),
        "C1": ((0, 0, 1), across, (0, 1, 1)),
        "F0": ((0, 1, 0), right, (-1, 1, 0)),
        "G0": ((0, 1, 0), left, (1, 1, 0)),
        "F1": ((0, 1, 1), right, (-1, 1, 1)),
        "G1": ((0, 1, 1), left, (1, 1, 1)),
        "D": ((-1, 0, 0), right, (2, 0, 0)),
        "E": ((1, 0, 1), left, (2, 0, 1)),
        "H": ((-1, 1, 0), right, (2, 1, 0)),
        "I": ((1, 1, 1), left, (2, 1, 1)),
    }
    send, recv = {}, {}
    for i, (name, (what, to, comes)) in enumerate(plan.items()):
        src = frames.at[pl.ds(64 * what[2], 64)] if what[:2] == (0, 0) else fr(*what)
        send[name] = gather_copy(i, src, fr(*what), to)
        recv[name] = gather_copy(i, fr(*comes), fr(*comes), to)
    for name in ("A0", "B1", "C0", "A1", "B0", "C1"):
        send[name].start()

    def kv_copies(b):
        return (
            remote(KV.at[b], H.at[base_sib + b], sib_s.at[b], sib_r.at[b], sibling),
            remote(KV.at[b], RL.at[b], off_s.at[b], off_r.at[b], relay),
        )

    def relay_copy(b):
        return remote(RL.at[b], H.at[base_off + b], rel_s.at[b], rel_r.at[b], relay_to)

    def project(b):
        r = jnp.dot(F[b], QW[...], preferred_element_type=F32).astype(BF)
        for hd in range(2):
            o = hd * 3 * HEAD_DIM
            cols = pl.ds(hd * HEAD_DIM, HEAD_DIM)
            Q[b, :, cols] = r[:, o : o + HEAD_DIM]
            KV[b, 0, :, cols] = r[:, o + HEAD_DIM : o + 2 * HEAD_DIM]
            KV[b, 1, :, cols] = r[:, o + 2 * HEAD_DIM : o + 3 * HEAD_DIM]
        to_sib, to_off = kv_copies(b)
        to_off.start()
        to_sib.start()

    def pass_on(dx, f):
        b = mod(x + dx, NX) * 2 + lax.rem(1 - yl + f, 2)
        remote(RL.at[b], RL.at[b], off_s.at[b], off_r.at[b], relay).wait_recv()
        relay_copy(b).start()

    def wz(s, up):
        return mod(z - s, NZ) if up else mod(z + s, NZ)

    def w_set(zs, part):
        return W.at[pl.ds(*part), zs, c]

    FULL, UPART, DPART = (1, 7), (1, 4), (5, 3)

    def w_send(s, up):
        zs = wz(s - 1, up)
        part = FULL if s < 4 else (UPART if up else DPART)
        ref = w_set(zs, part)
        if up:
            return remote(ref, ref, wu_s.at[s], wu_r.at[s], above)
        return remote(ref, ref, wd_s.at[s], wd_r.at[s], below)

    def w_recv(s, up):
        zs = wz(s, up)
        part = FULL if s < 4 else (UPART if up else DPART)
        ref = w_set(zs, part)
        if up:
            return remote(ref, ref, wu_s.at[s], wu_r.at[s], above)
        return remote(ref, ref, wd_s.at[s], wd_r.at[s], below)

    def w_sib(j):
        ref = w_set(mod(z + j, NZ), FULL)
        return remote(ref, ref, ws_s.at[j], ws_r.at[j], sibling)

    def w_sib_recv(j):
        ref = W.at[pl.ds(*FULL), mod(z + j, NZ), 1 - c]
        return remote(ref, ref, ws_s.at[j], ws_r.at[j], sibling)

    def w_step(s):
        w_recv(s, True).wait_recv()
        w_send(s + 1, True).start()
        w_recv(s, False).wait_recv()
        w_send(s + 1, False).start()
        w_sib(8 - s).start()
        w_sib(s).start()

    load_own.wait()
    load_qw.wait()
    project(head)
    load_w.wait()

    for k in range(1, 8):
        ref = W.at[k, z, c, :, mine]
        remote(ref, ref, wp_s.at[k], wp_r.at[k], across).wait_recv()
    for i, (a, b, n) in enumerate(((0, 4, 4), (5, 1, 3))):
        src, dst = W.at[pl.ds(a, n), z, c, :, mine], W.at[pl.ds(b, n), z, c, :, mine]
        remote(src, dst, wx_s.at[i], wx_r.at[i], relay).start()

    def w_swap(i):
        b, n = ((4, 4), (1, 3))[i]
        ref = W.at[pl.ds(b, n), z, c, :, other]
        return remote(ref, ref, wx_s.at[i], wx_r.at[i], relay)

    for k in range(1, 8):
        dx, f = rels[k]
        row = IDS.at[block(dx, f)]
        remote(row, row, id_s.at[k], id_r.at[k], across).wait_recv()
    ids_sib = remote(IDS, HID.at[pl.ds(base_sib, 8)], hid_s.at[0], hid_r.at[0], sibling)
    ids_off = remote(IDS, RID, hid_s.at[1], hid_r.at[1], relay)
    ids_rel = remote(RID, HID.at[pl.ds(base_off, 8)], hid_s.at[2], hid_r.at[2], relay_to)
    ids_off.start()
    ids_sib.start()
    for b in range(8):
        QID[b] = jnp.transpose(jnp.broadcast_to(IDS[b], (128, 128)))

    recv["C0"].wait_recv()
    send["F0"].start()
    send["G0"].start()
    w_swap(0).wait_recv()
    w_swap(1).wait_recv()
    w_send(1, True).start()
    w_send(1, False).start()
    w_sib(0).start()
    pass_on(0, 0)
    recv["C1"].wait_recv()
    send["F1"].start()
    send["G1"].start()
    project(block(0, 1))
    recv["A0"].wait_recv()
    send["D"].start()
    recv["B1"].wait_recv()
    send["E"].start()
    recv["A1"].wait_recv()
    project(block(-1, 0))
    recv["B0"].wait_recv()
    project(block(1, 0))
    ids_off.wait_recv()
    ids_rel.start()
    pass_on(0, 1)
    pass_on(-1, 0)
    pass_on(1, 0)
    w_step(1)
    recv["F0"].wait_recv()
    send["H"].start()
    recv["G0"].wait_recv()
    recv["G1"].wait_recv()
    send["I"].start()
    recv["F1"].wait_recv()
    project(block(-1, 1))
    project(block(1, 1))
    recv["D"].wait_recv()
    recv["E"].wait_recv()
    project(block(2, 0))
    pass_on(-1, 1)
    pass_on(1, 1)
    w_step(2)
    recv["H"].wait_recv()
    recv["I"].wait_recv()
    project(block(2, 1))
    pass_on(2, 0)
    pass_on(2, 1)

    scale = HEAD_DIM ** (-0.5)
    dims = (((1,), (1,)), ((), ()))

    own_ids = jnp.concatenate([IDS[j] for j in range(8)], axis=1)

    def own_step(i, carry):
        qid = jnp.concatenate([QID[i]] * 8, axis=1)
        mask = qid == own_ids
        for hd in range(2):
            cols = pl.ds(hd * HEAD_DIM, HEAD_DIM)
            q = Q[i, :, cols]
            k = KV[:, 0, :, cols].reshape(1024, HEAD_DIM)
            v = KV[:, 1, :, cols].reshape(1024, HEAD_DIM)
            s = lax.dot_general(q, k, dims, preferred_element_type=F32) * scale
            s = jnp.where(mask, s, NEG)
            m = jnp.max(s, axis=1, keepdims=True)
            p = jnp.exp(s - m)
            M[i, hd] = m
            L[i, hd] = jnp.sum(p, axis=1, keepdims=True)
            A[i, hd] = jnp.dot(p.astype(BF), v, preferred_element_type=F32)
        return carry

    lax.fori_loop(0, 8, own_step, 0)

    w_step(3)

    for b in range(8):
        hs, ho = H.at[8 - base_sib + b], H.at[8 - base_off + b]
        remote(hs, hs, sib_s.at[b], sib_r.at[b], sibling).wait_recv()
        remote(ho, ho, rel_s.at[b], rel_r.at[b], sibling).wait_recv()
    hs, ho = HID.at[pl.ds(8 - base_sib, 8)], HID.at[pl.ds(8 - base_off, 8)]
    remote(hs, hs, hid_s.at[0], hid_r.at[0], sibling).wait_recv()
    remote(ho, ho, hid_s.at[2], hid_r.at[2], sibling).wait_recv()

    def halo_step(t, carry):
        d = 7 - t
        dx = lax.rem(d, NX)
        f = d // NX
        i = block(dx, f)
        kid = jnp.concatenate([HID[i + j] for j in range(9)], axis=1)
        qid = jnp.concatenate([QID[i]] * 9, axis=1)
        mask = qid == kid
        for hd in range(2):
            cols = pl.ds(hd * HEAD_DIM, HEAD_DIM)
            q = Q[i, :, cols]
            k = H[pl.ds(i, 9), 0, :, cols].reshape(9 * 128, HEAD_DIM)
            v = H[pl.ds(i, 9), 1, :, cols].reshape(9 * 128, HEAD_DIM)
            s = lax.dot_general(q, k, dims, preferred_element_type=F32) * scale
            s = jnp.where(mask, s, NEG)
            m0 = M[i, hd]
            m = jnp.maximum(m0, jnp.max(s, axis=1, keepdims=True))
            p = jnp.exp(s - m)
            decay = jnp.exp(m0 - m)
            total = L[i, hd] * decay + jnp.sum(p, axis=1, keepdims=True)
            mixed = A[i, hd] * decay + jnp.dot(p.astype(BF), v, preferred_element_type=F32)
            ATS[d, :, cols] = (mixed / total).astype(BF)
        back = f * NX + mod(-dx, NX)

        @pl.when(d > 0)
        def _():
            remote(ATS.at[d], ATR.at[back], at_s.at[d], at_r.at[back], (blk, i)).start()

        return carry

    lax.fori_loop(0, 8, halo_step, 0)

    w_recv(4, True).wait_recv()
    w_recv(4, False).wait_recv()
    w_sib(4).start()
    for j in range(8):
        w_sib_recv(j).wait_recv()

    def out_part(a, d):
        return jnp.dot(a, W[d].reshape(256, 2048), preferred_element_type=F32)

    ACC[...] = out_part(ATS[0], 0)

    def out_step(t, carry):
        d = 7 - t
        remote(ATR.at[d], ATR.at[d], at_s.at[d], at_r.at[d], sibling).wait_recv()
        ACC[...] += out_part(ATR[d], d)
        return carry

    lax.fori_loop(0, 7, out_step, 0)
    out[...] = ACC[...].astype(BF)

    for k in range(1, 8):
        piece[k].wait_send()
        idc[k].wait_send()
        remote(ATS.at[k], ATR.at[k], at_s.at[k], at_r.at[k], sibling).wait_send()
    for name in plan:
        send[name].wait_send()
    for i, (a, n) in enumerate(((0, 4), (5, 3))):
        ref = W.at[pl.ds(a, n), z, c, :, mine]
        remote(ref, ref, wx_s.at[i], wx_r.at[i], relay).wait_send()
    for b in range(8):
        to_sib, to_off = kv_copies(b)
        to_sib.wait_send()
        to_off.wait_send()
        relay_copy(b).wait_send()
        w_sib(b).wait_send()
    ids_sib.wait_send()
    ids_off.wait_send()
    ids_rel.wait_send()
    for s in range(1, 5):
        w_send(s, True).wait_send()
        w_send(s, False).wait_send()


def shards(frames, qkv_weight, out_weight, recording):
    dma = pltpu.SemaphoreType.DMA
    any_ = pl.BlockSpec(memory_space=pl.ANY)
    vmem = pl.BlockSpec(memory_space=pltpu.VMEM)
    V = pltpu.VMEM
    return pl.pallas_call(
        kernel,
        name="encoder_block",
        out_shape=jax.ShapeDtypeStruct((128, 2048), BF),
        in_specs=[any_, any_, any_, vmem],
        out_specs=vmem,
        scratch_shapes=[
            V((8, 128, 2048), BF),
            V((2048, 768), BF),
            V((8, 8, 2, 16, 2048), BF),
            V((8, 128, 256), BF),
            V((8, 2, 128, 256), BF),
            V((16, 2, 128, 256), BF),
            V((8, 2, 128, 256), BF),
            V((8, 1, 128), jnp.int32),
            V((16, 1, 128), jnp.int32),
            V((8, 1, 128), jnp.int32),
            V((8, 128, 128), jnp.int32),
            V((8, 128, 256), BF),
            V((8, 128, 256), BF),
            V((128, 2048), F32),
            V((8, 2, 128, 1), F32),
            V((8, 2, 128, 1), F32),
            V((8, 2, 128, 128), F32),
            dma((3,)),
            dma((14,)), dma((14,)),
            dma((8,)), dma((8,)),
            dma((3,)), dma((3,)),
            dma((8,)), dma((8,)),
            dma((8,)), dma((8,)),
            dma((8,)), dma((8,)),
            dma((8,)), dma((8,)),
            dma((2,)), dma((2,)),
            dma((5,)), dma((5,)),
            dma((5,)), dma((5,)),
            dma((8,)), dma((8,)),
            dma((8,)), dma((8,)),
        ],
        compiler_params=pltpu.CompilerParams(
            collective_id=0, has_side_effects=True, vmem_limit_bytes=56 * 2**20
        ),
    )(frames, qkv_weight, out_weight.reshape(8, 2, 16, 2048), recording.reshape(1, 128))


def solution(mesh):
    in_specs = (P(("blk", "head"), None), P(None, "head"), P("head", None), P(("blk", "head")))
    out_specs = P(("blk", "head"), None)
    return jax.shard_map(shards, mesh=mesh, in_specs=in_specs, out_specs=out_specs, check_vma=False)
```

```python
import functools

import jax
import jax.numpy as jnp
from jax import lax
from jax.experimental import pallas as pl
from jax.experimental.pallas import tpu as pltpu
from jax.sharding import PartitionSpec as P

HEAD_DIM = 128
MESH = pl.DeviceIdType.MESH
NX, NZ, NB = 4, 8, 32
BF = jnp.bfloat16
F32 = jnp.float32
NEG = -jnp.inf


def mod(a, n):
    return lax.rem(a + 2 * n, n)


def kernel(
    frames, qw_in, ow, ids, out,
    F, QW, W, Q, KV, H, RL, IDS, HID, RID, QID, ATS, ATR, ACC, M, L, A,
    loc, ag_s, ag_r, id_s, id_r, hid_s, hid_r, sib_s, sib_r, off_s, off_r, rel_s, rel_r,
    wp_s, wp_r, wx_s, wx_r, wu_s, wu_r, wd_s, wd_r, ws_s, ws_r, at_s, at_r,
):
    blk = lax.axis_index("blk")
    head = lax.axis_index("head")
    z = blk // 4
    yh = lax.rem(blk, 4) // 2
    c = lax.rem(blk, 2)
    x = head // 2
    yl = lax.rem(head, 2)

    def block(dx, f):
        return mod(x + dx, NX) * 2 + lax.rem(yl + f, 2)

    def peer(dx, f):
        return (blk, block(dx, f))

    right, left, across = peer(1, 0), peer(-1, 0), peer(0, 1)
    sibling = (blk + 1 - 2 * c, head)
    lean = 1 - 2 * yh
    ahead = (mod(blk + 4 * lean, NB), head)
    behind = (mod(blk - 4 * lean, NB), head)
    owner_blk = z * 4 + (1 - yh) * 2 + c
    owner_head = x * 2 + 1 - yl
    relay = (owner_blk, owner_head)
    relay_to = (mod(owner_blk + 2 * c - 1, NB), owner_head)
    far = mod(blk + 2 * c - 1, NB)
    relay_from = ((far // 4) * 4 + (1 - lax.rem(far, 4) // 2) * 2 + lax.rem(far, 2), owner_head)
    base_off = 8 * (1 - c)
    base_sib = 8 * c

    def remote(src, dst, ss, rs, dev):
        return pltpu.make_async_remote_copy(
            src_ref=src, dst_ref=dst, send_sem=ss, recv_sem=rs, device_id=dev, device_id_type=MESH
        )

    load_qw = pltpu.make_async_copy(qw_in, QW, loc.at[0])
    load_own = pltpu.make_async_copy(frames, F.at[head], loc.at[1])
    load_w = pltpu.make_async_copy(ow, W.at[0], loc.at[2])
    load_own.start()
    load_qw.start()
    load_w.start()
    rels = [(dx, f) for f in range(2) for dx in range(NX)]
    partners = [peer(dx, f) for dx, f in rels[1:]]
    partners += [sibling, ahead, behind, relay, relay_to, relay_from, (far, head)]
    barrier = pltpu.get_barrier_semaphore()
    for p in partners:
        pl.semaphore_signal(barrier, inc=1, device_id=p, device_id_type=MESH)
    pl.semaphore_wait(barrier, len(partners))

    idc = [None]
    for k in range(1, 8):
        dx, f = rels[k]
        back = f * NX + (-dx) % NX
        idc.append(remote(ids, IDS.at[head], id_s.at[k], id_r.at[back], peer(dx, f)))
        idc[k].start()
    IDS[head] = ids[...]

    def w_piece(dx, s, i):
        zs = mod(z + s * lean, NZ)
        back = (-dx) % NX
        return remote(ow.at[zs, c], W.at[back, zs, c], wp_s.at[5 * dx + i], wp_r.at[5 * back + i], peer(dx, 0))

    def w_piece_wait(dx, s, i):
        ref = W.at[dx, mod(z + s * lean, NZ), c]
        remote(ref, ref, wp_s.at[5 * dx + i], wp_r.at[5 * dx + i], right).wait_recv()

    for dx in (1, 3, 2):
        w_piece(dx, 0, 0).start()

    def fr(dx, f, start, rows=64):
        return F.at[block(dx, f), pl.ds(start, rows)]

    def gather_copy(i, src, dst, dev):
        return remote(src, dst, ag_s.at[i], ag_r.at[i], dev)

    plan = {
        "A0": ((0, 0, 0), right, (-1, 0, 0)),
        "B1": ((0, 0, 64), left, (1, 0, 64)),
        "C0": ((0, 0, 0), across, (0, 1, 0)),
        "A1": ((0, 0, 64), right, (-1, 0, 64)),
        "B0": ((0, 0, 0), left, (1, 0, 0)),
        "C1": ((0, 0, 64), across, (0, 1, 64)),
        "F0": ((0, 1, 0), right, (-1, 1, 0)),
        "G0": ((0, 1, 32, 32), left, (1, 1, 32, 32)),
        "F1": ((0, 1, 64, 32), right, (-1, 1, 64, 32)),
        "G1": ((0, 1, 64), left, (1, 1, 64)),
        "J": ((-1, 0, 96, 32), across, (-1, 1, 96, 32)),
        "K": ((1, 0, 0, 32), across, (1, 1, 0, 32)),
        "D": ((-1, 0, 0), right, (2, 0, 0)),
        "E": ((1, 0, 64), left, (2, 0, 64)),
        "H": ((-1, 1, 0), right, (2, 1, 0)),
        "I": ((1, 1, 64), left, (2, 1, 64)),
    }
    send, recv = {}, {}
    for i, (name, (what, to, comes)) in enumerate(plan.items()):
        src = frames.at[pl.ds(what[2], 64)] if what[:2] == (0, 0) else fr(*what)
        send[name] = gather_copy(i, src, fr(*what), to)
        recv[name] = gather_copy(i, fr(*comes), fr(*comes), to)
    send["C0"].start()

    def sib_copy(b):
        return remote(KV.at[b], H.at[base_sib + b], sib_s.at[b], sib_r.at[b], sibling)

    def off_copy(b):
        return remote(KV.at[b], RL.at[b], off_s.at[b], off_r.at[b], relay)

    def direct_copy(b):
        return remote(KV.at[b], H.at[base_off + b], off_s.at[b], rel_r.at[b], (far, head))

    def relay_copy(b):
        return remote(RL.at[b], H.at[base_off + b], rel_s.at[b], rel_r.at[b], relay_to)

    def project(b, direct=False):
        r = jnp.dot(F[b], QW[...], preferred_element_type=F32).astype(BF)
        for hd in range(2):
            o = hd * 3 * HEAD_DIM
            cols = pl.ds(hd * HEAD_DIM, HEAD_DIM)
            Q[b, :, cols] = r[:, o : o + HEAD_DIM]
            KV[b, 0, :, cols] = r[:, o + HEAD_DIM : o + 2 * HEAD_DIM]
            KV[b, 1, :, cols] = r[:, o + 2 * HEAD_DIM : o + 3 * HEAD_DIM]
        (direct_copy(b) if direct else off_copy(b)).start()
        sib_copy(b).start()

    def pass_on(dx, f):
        b = mod(x + dx, NX) * 2 + lax.rem(1 - yl + f, 2)
        remote(RL.at[b], RL.at[b], off_s.at[b], off_r.at[b], relay).wait_recv()
        relay_copy(b).start()

    PART = ((1, 3), (4, 4))
    STEPS = {(0, True): 1, (0, False): 2, (1, True): 3, (1, False): 4}

    def w_set(s, part, core):
        return W.at[pl.ds(*PART[part]), mod(z + s * lean, NZ), core]

    def w_copy(ref, s, part, leaning):
        i = part * 5 + s
        if leaning:
            return remote(ref, ref, wu_s.at[i], wu_r.at[i], ahead)
        return remote(ref, ref, wd_s.at[i], wd_r.at[i], behind)

    def w_send(s, part, leaning):
        return w_copy(w_set((1 - s) if leaning else (s - 1), part, c), s, part, leaning)

    def w_recv(s, part, leaning):
        return w_copy(w_set(-s if leaning else s, part, c), s, part, leaning)

    def w_sib(j, part):
        ref = w_set(j, part, c)
        return remote(ref, ref, ws_s.at[part * 8 + j], ws_r.at[part * 8 + j], sibling)

    def w_sib_recv(j, part):
        ref = w_set(j, part, 1 - c)
        return remote(ref, ref, ws_s.at[part * 8 + j], ws_r.at[part * 8 + j], sibling)

    def w_first(part):
        w_send(1, part, True).start()
        w_send(1, part, False).start()
        w_sib(0, part).start()

    def w_step(s, part, leaning):
        w_recv(s, part, leaning).wait_recv()
        if s < STEPS[part, leaning]:
            w_send(s + 1, part, leaning).start()
        w_sib(8 - s if leaning else s, part).start()

    w_swap = remote(W.at[pl.ds(0, 4), z, c], W.at[pl.ds(4, 4), z, c], wx_s.at[0], wx_r.at[0], relay)

    load_own.wait()
    load_qw.wait()
    for dx in (1, 3, 2):
        w_piece(dx, 0, 0).wait_send()
    for name in ("A0", "B1", "A1", "B0", "C1"):
        send[name].start()
    project(head)
    load_w.wait()
    for dx in (1, 3, 2):
        w_piece_wait(dx, 0, 0)
    w_swap.start()
    w_first(0)

    for k in range(1, 8):
        dx, f = rels[k]
        row = IDS.at[block(dx, f)]
        remote(row, row, id_s.at[k], id_r.at[k], across).wait_recv()
    ids_sib = remote(IDS, HID.at[pl.ds(base_sib, 8)], hid_s.at[0], hid_r.at[0], sibling)
    ids_off = remote(IDS, RID, hid_s.at[1], hid_r.at[1], relay)
    ids_rel = remote(RID, HID.at[pl.ds(base_off, 8)], hid_s.at[2], hid_r.at[2], relay_to)
    ids_off.start()
    ids_sib.start()
    for b in range(8):
        QID[b] = jnp.transpose(jnp.broadcast_to(IDS[b], (128, 128)))

    scale = HEAD_DIM ** (-0.5)
    dims = (((1,), (1,)), ((), ()))

    def attend(dx, chunks, first, last):
        a = mod(x + dx, NX)
        q_at = pl.ds(2 * a, 2)
        qid = QID[q_at].reshape(256, 128)
        kid = jnp.concatenate([r[b + j] for _, r, b in chunks for j in range(2)], axis=1)
        mask = jnp.concatenate([qid] * (2 * len(chunks)), axis=1) == kid
        for hd in range(2):
            cols = pl.ds(hd * HEAD_DIM, HEAD_DIM)
            q = Q[q_at, :, cols].reshape(256, HEAD_DIM)
            k, v = (
                jnp.concatenate([r[pl.ds(b, 2), n, :, cols].reshape(256, HEAD_DIM) for r, _, b in chunks], axis=0)
                for n in range(2)
            )
            s = lax.dot_general(q, k, dims, preferred_element_type=F32) * scale
            s = jnp.where(mask, s, NEG)
            m = jnp.max(s, axis=1, keepdims=True)
            if not first:
                m0 = M[a, hd]
                m = jnp.maximum(m0, m)
                decay = jnp.exp(m0 - m)
            p = jnp.exp(s - m)
            total = jnp.sum(p, axis=1, keepdims=True)
            mixed = jnp.dot(p.astype(BF), v, preferred_element_type=F32)
            if not first:
                total = L[a, hd] * decay + total
                mixed = A[a, hd] * decay + mixed
            if last:
                mixed = (mixed / total).astype(BF)
                for f in range(2):
                    rel = lax.rem(yl + f, 2) * NX + dx
                    ATS[rel, :, cols] = mixed[128 * f : 128 * (f + 1)]
            else:
                M[a, hd] = m
                L[a, hd] = total
                A[a, hd] = mixed

    def own(dx):
        return (KV, IDS, 2 * mod(x + dx, NX))

    def halo(dx, side):
        return (H, HID, 8 * side + 2 * mod(x + dx, NX))

    def facing(dx, key_dx):
        side = jnp.where(mod(x + key_dx, NX) >= mod(x + dx, NX), 0, 1)
        return halo(key_dx, side)

    near = (0, 1, -1)

    def each_near(body):
        def step(t, carry):
            body(lax.rem(3 + t, NX))
            return carry

        lax.fori_loop(0, 3, step, 0)

    def halo_wait(dx, f):
        b = block(dx, f)
        hs, ho = H.at[8 - base_sib + b], H.at[8 - base_off + b]
        remote(hs, hs, sib_s.at[b], sib_r.at[b], sibling).wait_recv()
        remote(ho, ho, rel_s.at[b], rel_r.at[b], sibling).wait_recv()

    pass_on(0, 0)
    w_step(1, 0, False)
    w_step(1, 0, True)
    w_swap.wait_recv()
    w_first(1)
    recv["C0"].wait_recv()
    send["F0"].start()
    send["G0"].start()
    recv["C1"].wait_recv()
    send["F1"].start()
    send["G1"].start()
    project(block(0, 1))
    recv["A0"].wait_recv()
    recv["A1"].wait_recv()
    send["J"].start()
    recv["B1"].wait_recv()
    recv["B0"].wait_recv()
    send["K"].start()
    project(block(-1, 0))
    project(block(1, 0))
    w_step(1, 1, True)
    w_step(2, 0, False)
    w_step(1, 1, False)
    pass_on(0, 1)
    ids_off.wait_recv()
    ids_rel.start()
    send["F1"].wait_send()
    send["D"].start()
    send["G1"].wait_send()
    send["E"].start()
    recv["F0"].wait_recv()
    send["H"].start()
    recv["G1"].wait_recv()
    send["I"].start()
    recv["G0"].wait_recv()
    recv["K"].wait_recv()
    project(block(1, 1))
    recv["F1"].wait_recv()
    recv["J"].wait_recv()
    project(block(-1, 1))
    pass_on(-1, 0)
    pass_on(1, 0)
    w_step(2, 1, True)
    attend(0, [own(n) for n in near], True, False)
    attend(1, [own(n) for n in near], True, False)
    w_step(2, 1, False)
    attend(3, [own(n) for n in near], True, False)
    pass_on(1, 1)
    pass_on(-1, 1)
    for name in ("D", "E", "H", "I"):
        send[name].wait_send()
    for i in range(4):
        for dx in (1, 3, 2):
            w_piece(dx, 3 + i, 1 + i).start()
    recv["D"].wait_recv()
    recv["E"].wait_recv()
    project(block(2, 0))
    recv["H"].wait_recv()
    recv["I"].wait_recv()
    project(block(2, 1), direct=True)
    w_step(3, 1, False)
    w_step(3, 1, True)
    pass_on(2, 0)

    hs, ho = HID.at[pl.ds(8 - base_sib, 8)], HID.at[pl.ds(8 - base_off, 8)]
    remote(hs, hs, hid_s.at[0], hid_r.at[0], sibling).wait_recv()
    remote(ho, ho, hid_s.at[2], hid_r.at[2], sibling).wait_recv()
    for dx in near:
        for f in range(2):
            halo_wait(dx, f)
    attend(2, [own(n) for n in near] + [own(2)] + [facing(2, n) for n in near], True, False)
    w_step(4, 1, False)
    each_near(lambda dx: attend(dx, [own(2)] + [facing(dx, n) for n in near] + [halo(dx, 1)], False, False))
    for i in range(4):
        for dx in (1, 3, 2):
            w_piece_wait(dx, 3 + i, 1 + i)
        w_sib(3 + i, 0).start()
    halo_wait(2, 0)
    halo_wait(2, 1)

    def hand_over(dx):
        for f in range(2):
            rel = f * NX + dx
            back = f * NX + mod(-dx, NX)

            @pl.when(rel > 0)
            def _():
                remote(ATS.at[rel], ATR.at[back], at_s.at[rel], at_r.at[back], peer(dx, f)).start()

    def finish(dx, chunks):
        attend(dx, chunks, False, True)
        hand_over(dx)

    finish(2, [halo(2, 0), halo(2, 1)])
    each_near(lambda dx: finish(dx, [facing(dx, 2)]))

    for j in range(8):
        w_sib_recv(j, 0).wait_recv()
        w_sib_recv(j, 1).wait_recv()

    def out_part(a, d):
        return jnp.dot(a, W[d].reshape(256, 2048), preferred_element_type=F32)

    ACC[...] = out_part(ATS[0], 0)

    def out_step(t, carry):
        d = lax.rem(2 + 4 * t, 7) + jnp.where(lax.rem(2 + 4 * t, 7) == 0, 7, 0)
        remote(ATR.at[d], ATR.at[d], at_s.at[d], at_r.at[d], sibling).wait_recv()
        ACC[...] += out_part(ATR[d], d)
        return carry

    lax.fori_loop(0, 7, out_step, 0)
    out[...] = ACC[...].astype(BF)

    for k in range(1, 8):
        idc[k].wait_send()
        remote(ATS.at[k], ATR.at[k], at_s.at[k], at_r.at[k], sibling).wait_send()
    for name in plan:
        if name not in ("F1", "G1", "D", "E", "H", "I"):
            send[name].wait_send()
    for i in range(4):
        for dx in (1, 3, 2):
            w_piece(dx, 3 + i, 1 + i).wait_send()
    w_swap.wait_send()
    for b in range(8):
        sib_copy(b).wait_send()
        off_copy(b).wait_send()
        w_sib(b, 0).wait_send()
        w_sib(b, 1).wait_send()
    for k in range(7):
        dx, f = ((0, 0), (0, 1), (-1, 0), (1, 0), (-1, 1), (1, 1), (2, 0))[k]
        relay_copy(mod(x + dx, NX) * 2 + lax.rem(1 - yl + f, 2)).wait_send()
    ids_sib.wait_send()
    ids_off.wait_send()
    ids_rel.wait_send()
    for (part, leaning), n in STEPS.items():
        for s in range(1, n + 1):
            w_send(s, part, leaning).wait_send()


def shards(frames, qkv_weight, out_weight, recording):
    dma = pltpu.SemaphoreType.DMA
    any_ = pl.BlockSpec(memory_space=pl.ANY)
    vmem = pl.BlockSpec(memory_space=pltpu.VMEM)
    V = pltpu.VMEM
    return pl.pallas_call(
        kernel,
        name="encoder_block",
        out_shape=jax.ShapeDtypeStruct((128, 2048), BF),
        in_specs=[any_, any_, any_, vmem],
        out_specs=vmem,
        scratch_shapes=[
            V((8, 128, 2048), BF),
            V((2048, 768), BF),
            V((8, 8, 2, 16, 2048), BF),
            V((8, 128, 256), BF),
            V((8, 2, 128, 256), BF),
            V((16, 2, 128, 256), BF),
            V((8, 2, 128, 256), BF),
            V((8, 1, 128), jnp.int32),
            V((16, 1, 128), jnp.int32),
            V((8, 1, 128), jnp.int32),
            V((8, 128, 128), jnp.int32),
            V((8, 128, 256), BF),
            V((8, 128, 256), BF),
            V((128, 2048), F32),
            V((4, 2, 256, 1), F32),
            V((4, 2, 256, 1), F32),
            V((4, 2, 256, 128), F32),
            dma((3,)),
            dma((16,)), dma((16,)),
            dma((8,)), dma((8,)),
            dma((3,)), dma((3,)),
            dma((8,)), dma((8,)),
            dma((8,)), dma((8,)),
            dma((8,)), dma((8,)),
            dma((20,)), dma((20,)),
            dma((1,)), dma((1,)),
            dma((10,)), dma((10,)),
            dma((10,)), dma((10,)),
            dma((16,)), dma((16,)),
            dma((8,)), dma((8,)),
        ],
        compiler_params=pltpu.CompilerParams(
            collective_id=0, has_side_effects=True, vmem_limit_bytes=56 * 2**20
        ),
    )(frames, qkv_weight, out_weight.reshape(8, 2, 16, 2048), recording.reshape(1, 128))


def solution(mesh):
    in_specs = (P(("blk", "head"), None), P(None, "head"), P("head", None), P(("blk", "head")))
    out_specs = P(("blk", "head"), None)
    return jax.shard_map(shards, mesh=mesh, in_specs=in_specs, out_specs=out_specs, check_vma=False)
```

```python
import functools

import jax
import jax.numpy as jnp
from jax import lax
from jax.experimental import pallas as pl
from jax.experimental.pallas import tpu as pltpu
from jax.sharding import PartitionSpec as P

HEAD_DIM = 128
MESH = pl.DeviceIdType.MESH
NX, NZ, NB = 4, 8, 32
BF = jnp.bfloat16
F32 = jnp.float32
NEG = -jnp.inf


def mod(a, n):
    return lax.rem(a + 2 * n, n)


def kernel(
    frames, qw_in, ow, ids, out,
    F, QW, W, Q, KV, H, RL, IDS, HID, RID, QID, ATS, ATR, ACC, M, L, A,
    loc, ag_s, ag_r, id_s, id_r, hid_s, hid_r, sib_s, sib_r, off_s, off_r, rel_s, rel_r,
    wp_s, wp_r, wx_s, wx_r, wu_s, wu_r, wd_s, wd_r, ws_s, ws_r, at_s, at_r,
):
    blk = lax.axis_index("blk")
    head = lax.axis_index("head")
    z = blk // 4
    yh = lax.rem(blk, 4) // 2
    c = lax.rem(blk, 2)
    x = head // 2
    yl = lax.rem(head, 2)

    def block(dx, f):
        return mod(x + dx, NX) * 2 + lax.rem(yl + f, 2)

    def peer(dx, f):
        return (blk, block(dx, f))

    right, left, across = peer(1, 0), peer(-1, 0), peer(0, 1)
    sibling = (blk + 1 - 2 * c, head)
    lean = 1 - 2 * yh
    ahead = (mod(blk + 4 * lean, NB), head)
    behind = (mod(blk - 4 * lean, NB), head)
    owner_blk = z * 4 + (1 - yh) * 2 + c
    owner_head = x * 2 + 1 - yl
    relay = (owner_blk, owner_head)
    relay_to = (mod(owner_blk + 2 * c - 1, NB), owner_head)
    far = mod(blk + 2 * c - 1, NB)
    relay_from = ((far // 4) * 4 + (1 - lax.rem(far, 4) // 2) * 2 + lax.rem(far, 2), owner_head)
    base_off = 8 * (1 - c)
    base_sib = 8 * c

    def remote(src, dst, ss, rs, dev):
        return pltpu.make_async_remote_copy(
            src_ref=src, dst_ref=dst, send_sem=ss, recv_sem=rs, device_id=dev, device_id_type=MESH
        )

    load_qw = pltpu.make_async_copy(qw_in, QW, loc.at[0])
    load_own = pltpu.make_async_copy(frames, F.at[head], loc.at[1])
    load_w = pltpu.make_async_copy(ow, W.at[0], loc.at[2])
    load_own.start()
    load_qw.start()
    load_w.start()
    rels = [(dx, f) for f in range(2) for dx in range(NX)]
    partners = [peer(dx, f) for dx, f in rels[1:]]
    partners += [sibling, ahead, behind, relay, relay_to, relay_from, (far, head)]
    barrier = pltpu.get_barrier_semaphore()
    for p in partners:
        pl.semaphore_signal(barrier, inc=1, device_id=p, device_id_type=MESH)
    pl.semaphore_wait(barrier, len(partners))

    idc = [None]
    for k in range(1, 8):
        dx, f = rels[k]
        back = f * NX + (-dx) % NX
        idc.append(remote(ids, IDS.at[head], id_s.at[k], id_r.at[back], peer(dx, f)))
        idc[k].start()
    IDS[head] = ids[...]

    def w_piece(dx, s, i):
        zs = mod(z + s * lean, NZ)
        back = (-dx) % NX
        return remote(ow.at[zs, c], W.at[back, zs, c], wp_s.at[5 * dx + i], wp_r.at[5 * back + i], peer(dx, 0))

    def w_piece_wait(dx, s, i):
        ref = W.at[dx, mod(z + s * lean, NZ), c]
        remote(ref, ref, wp_s.at[5 * dx + i], wp_r.at[5 * dx + i], right).wait_recv()

    for dx in (1, 3, 2):
        w_piece(dx, 0, 0).start()
    w_own = remote(ow.at[z, c], W.at[4, z, c], wx_s.at[1], wx_r.at[1], relay)
    w_own.start()

    def fr(dx, f, start, rows=64):
        return F.at[block(dx, f), pl.ds(start, rows)]

    def gather_copy(i, src, dst, dev):
        return remote(src, dst, ag_s.at[i], ag_r.at[i], dev)

    plan = {
        "A0": ((0, 0, 0), right, (-1, 0, 0)),
        "B1": ((0, 0, 64), left, (1, 0, 64)),
        "C0": ((0, 0, 0), across, (0, 1, 0)),
        "A1": ((0, 0, 64), right, (-1, 0, 64)),
        "B0": ((0, 0, 0), left, (1, 0, 0)),
        "C1": ((0, 0, 64), across, (0, 1, 64)),
        "F0": ((0, 1, 0), right, (-1, 1, 0)),
        "G0": ((0, 1, 32, 32), left, (1, 1, 32, 32)),
        "F1": ((0, 1, 64, 32), right, (-1, 1, 64, 32)),
        "G1": ((0, 1, 64), left, (1, 1, 64)),
        "J": ((-1, 0, 96, 32), across, (-1, 1, 96, 32)),
        "K": ((1, 0, 0, 32), across, (1, 1, 0, 32)),
        "D": ((-1, 0, 0), right, (2, 0, 0)),
        "E": ((1, 0, 64), left, (2, 0, 64)),
        "H": ((-1, 1, 0), right, (2, 1, 0)),
        "I": ((1, 1, 64), left, (2, 1, 64)),
    }
    send, recv = {}, {}
    for i, (name, (what, to, comes)) in enumerate(plan.items()):
        src = frames.at[pl.ds(what[2], 64)] if what[:2] == (0, 0) else fr(*what)
        send[name] = gather_copy(i, src, fr(*what), to)
        recv[name] = gather_copy(i, fr(*comes), fr(*comes), to)
    send["C0"].start()

    def sib_copy(b):
        return remote(KV.at[b], H.at[base_sib + b], sib_s.at[b], sib_r.at[b], sibling)

    def off_copy(b):
        return remote(KV.at[b], RL.at[b], off_s.at[b], off_r.at[b], relay)

    def direct_copy(b):
        return remote(KV.at[b], H.at[base_off + b], off_s.at[b], rel_r.at[b], (far, head))

    def relay_copy(b):
        return remote(RL.at[b], H.at[base_off + b], rel_s.at[b], rel_r.at[b], relay_to)

    def project(b, direct=False):
        r = jnp.dot(F[b], QW[...], preferred_element_type=F32).astype(BF)
        for hd in range(2):
            o = hd * 3 * HEAD_DIM
            cols = pl.ds(hd * HEAD_DIM, HEAD_DIM)
            Q[b, :, cols] = r[:, o : o + HEAD_DIM]
            KV[b, 0, :, cols] = r[:, o + HEAD_DIM : o + 2 * HEAD_DIM]
            KV[b, 1, :, cols] = r[:, o + 2 * HEAD_DIM : o + 3 * HEAD_DIM]
        (direct_copy(b) if direct else off_copy(b)).start()
        sib_copy(b).start()

    def pass_on(dx, f):
        b = mod(x + dx, NX) * 2 + lax.rem(1 - yl + f, 2)
        remote(RL.at[b], RL.at[b], off_s.at[b], off_r.at[b], relay).wait_recv()
        relay_copy(b).start()

    PART = ((1, 3), (4, 4))
    STEPS = {(0, True): 1, (0, False): 3, (1, True): 3, (1, False): 4}

    def w_set(s, part, core):
        return W.at[pl.ds(*PART[part]), mod(z + s * lean, NZ), core]

    def w_copy(ref, s, part, leaning):
        i = part * 5 + s
        if leaning:
            return remote(ref, ref, wu_s.at[i], wu_r.at[i], ahead)
        return remote(ref, ref, wd_s.at[i], wd_r.at[i], behind)

    def w_send(s, part, leaning):
        return w_copy(w_set((1 - s) if leaning else (s - 1), part, c), s, part, leaning)

    def w_recv(s, part, leaning):
        return w_copy(w_set(-s if leaning else s, part, c), s, part, leaning)

    def w_sib(j, part):
        ref = w_set(j, part, c)
        return remote(ref, ref, ws_s.at[part * 8 + j], ws_r.at[part * 8 + j], sibling)

    def w_sib_recv(j, part):
        ref = w_set(j, part, 1 - c)
        return remote(ref, ref, ws_s.at[part * 8 + j], ws_r.at[part * 8 + j], sibling)

    def w_first(part):
        w_send(1, part, True).start()
        w_send(1, part, False).start()
        w_sib(0, part).start()

    def w_step(s, part, leaning):
        w_recv(s, part, leaning).wait_recv()
        if s < STEPS[part, leaning]:
            w_send(s + 1, part, leaning).start()
        w_sib(8 - s if leaning else s, part).start()

    w_swap = remote(W.at[pl.ds(1, 3), z, c], W.at[pl.ds(5, 3), z, c], wx_s.at[0], wx_r.at[0], relay)

    load_own.wait()
    load_qw.wait()
    for dx in (1, 3, 2):
        w_piece(dx, 0, 0).wait_send()
    for name in ("A0", "B1", "A1", "B0", "C1"):
        send[name].start()
    load_w.wait()
    for dx in (1, 3, 2):
        w_piece_wait(dx, 0, 0)
    w_swap.start()
    w_first(0)
    project(head)

    scale = HEAD_DIM ** (-0.5)
    dims = (((1,), (1,)), ((), ()))

    def attend(dx, chunks, first, last):
        a = mod(x + dx, NX)
        q_at = pl.ds(2 * a, 2)
        qid = QID[q_at].reshape(256, 128)
        kid = jnp.concatenate([r[b + j] for _, r, b in chunks for j in range(2)], axis=1)
        mask = jnp.concatenate([qid] * (2 * len(chunks)), axis=1) == kid
        for hd in range(2):
            cols = pl.ds(hd * HEAD_DIM, HEAD_DIM)
            q = Q[q_at, :, cols].reshape(256, HEAD_DIM)
            k, v = (
                jnp.concatenate([r[pl.ds(b, 2), n, :, cols].reshape(256, HEAD_DIM) for r, _, b in chunks], axis=0)
                for n in range(2)
            )
            s = lax.dot_general(q, k, dims, preferred_element_type=F32) * scale
            s = jnp.where(mask, s, NEG)
            m = jnp.max(s, axis=1, keepdims=True)
            if not first:
                m0 = M[a, hd]
                m = jnp.maximum(m0, m)
                decay = jnp.exp(m0 - m)
            p = jnp.exp(s - m)
            total = jnp.sum(p, axis=1, keepdims=True)
            mixed = jnp.dot(p.astype(BF), v, preferred_element_type=F32)
            if not first:
                total = L[a, hd] * decay + total
                mixed = A[a, hd] * decay + mixed
            if last:
                mixed = (mixed / total).astype(BF)
                for f in range(2):
                    rel = lax.rem(yl + f, 2) * NX + dx
                    ATS[rel, :, cols] = mixed[128 * f : 128 * (f + 1)]
            else:
                M[a, hd] = m
                L[a, hd] = total
                A[a, hd] = mixed

    def own(dx):
        return (KV, IDS, 2 * mod(x + dx, NX))

    def halo(dx, side):
        return (H, HID, 8 * side + 2 * mod(x + dx, NX))

    def facing(dx, key_dx):
        side = jnp.where(mod(x + key_dx, NX) >= mod(x + dx, NX), 0, 1)
        return halo(key_dx, side)

    near = (0, 1, -1)

    def each_near(body):
        def step(t, carry):
            body(lax.rem(3 + t, NX))
            return carry

        lax.fori_loop(0, 3, step, 0)

    def halo_wait(dx, f):
        b = block(dx, f)
        hs, ho = H.at[8 - base_sib + b], H.at[8 - base_off + b]
        remote(hs, hs, sib_s.at[b], sib_r.at[b], sibling).wait_recv()
        remote(ho, ho, rel_s.at[b], rel_r.at[b], sibling).wait_recv()

    def near_halo_wait(dx):
        if dx == 0:
            hs, ho = HID.at[pl.ds(8 - base_sib, 8)], HID.at[pl.ds(8 - base_off, 8)]
            remote(hs, hs, hid_s.at[0], hid_r.at[0], sibling).wait_recv()
            remote(ho, ho, hid_s.at[2], hid_r.at[2], sibling).wait_recv()
        halo_wait(dx, 0)
        halo_wait(dx, 1)

    w_step(1, 0, False)
    w_step(1, 0, True)
    w_own.wait_recv()
    w_swap.wait_recv()
    w_first(1)
    recv["C0"].wait_recv()
    send["F0"].start()
    send["G0"].start()
    recv["C1"].wait_recv()
    send["F1"].start()
    send["G1"].start()
    pass_on(0, 0)
    for k in range(1, 8):
        dx, f = rels[k]
        row = IDS.at[block(dx, f)]
        remote(row, row, id_s.at[k], id_r.at[k], across).wait_recv()
    ids_sib = remote(IDS, HID.at[pl.ds(base_sib, 8)], hid_s.at[0], hid_r.at[0], sibling)
    ids_off = remote(IDS, RID, hid_s.at[1], hid_r.at[1], relay)
    ids_rel = remote(RID, HID.at[pl.ds(base_off, 8)], hid_s.at[2], hid_r.at[2], relay_to)
    ids_off.start()
    ids_sib.start()
    for b in range(8):
        QID[b] = jnp.transpose(jnp.broadcast_to(IDS[b], (128, 128)))
    project(block(0, 1))
    recv["A0"].wait_recv()
    recv["A1"].wait_recv()
    send["J"].start()
    recv["B1"].wait_recv()
    recv["B0"].wait_recv()
    send["K"].start()
    project(block(-1, 0))
    project(block(1, 0))
    w_step(1, 1, True)
    w_step(2, 0, False)
    w_step(1, 1, False)
    pass_on(0, 1)
    ids_off.wait_recv()
    ids_rel.start()
    send["F1"].wait_send()
    send["D"].start()
    send["G1"].wait_send()
    send["E"].start()
    recv["F0"].wait_recv()
    send["H"].start()
    recv["G1"].wait_recv()
    send["I"].start()
    recv["G0"].wait_recv()
    recv["K"].wait_recv()
    project(block(1, 1))
    recv["F1"].wait_recv()
    recv["J"].wait_recv()
    project(block(-1, 1))
    pass_on(-1, 0)
    pass_on(1, 0)
    w_step(2, 1, True)
    near_halo_wait(0)
    each_near(lambda dx: attend(dx, [own(n) for n in near] + [facing(dx, 0)], True, False))
    w_step(2, 1, False)
    w_step(3, 0, False)
    pass_on(1, 1)
    pass_on(-1, 1)
    for name in ("D", "E", "H", "I"):
        send[name].wait_send()
    for i in range(3):
        for dx in (1, 3, 2):
            w_piece(dx, 4 + i, 1 + i).start()
    recv["D"].wait_recv()
    recv["E"].wait_recv()
    project(block(2, 0))
    recv["H"].wait_recv()
    recv["I"].wait_recv()
    project(block(2, 1), direct=True)
    attend(2, [own(n) for n in near] + [own(2)], True, False)
    pass_on(2, 0)
    w_step(3, 1, False)
    near_halo_wait(1)
    near_halo_wait(-1)
    each_near(lambda dx: attend(dx, [own(2), facing(dx, 1), facing(dx, -1), halo(dx, 1)], False, False))
    w_step(3, 1, True)
    attend(2, [facing(2, n) for n in near], False, False)
    w_step(4, 1, False)
    for i in range(3):
        for dx in (1, 3, 2):
            w_piece_wait(dx, 4 + i, 1 + i)
        w_sib(4 + i, 0).start()
    halo_wait(2, 0)
    halo_wait(2, 1)

    def hand_over(dx):
        for f in range(2):
            rel = f * NX + dx
            back = f * NX + mod(-dx, NX)

            @pl.when(rel > 0)
            def _():
                remote(ATS.at[rel], ATR.at[back], at_s.at[rel], at_r.at[back], peer(dx, f)).start()

    def finish(dx, chunks):
        attend(dx, chunks, False, True)
        hand_over(dx)

    finish(2, [halo(2, 0), halo(2, 1)])
    each_near(lambda dx: finish(dx, [facing(dx, 2)]))

    for j in range(8):
        w_sib_recv(j, 0).wait_recv()
        w_sib_recv(j, 1).wait_recv()

    def out_part(a, d):
        return jnp.dot(a, W[d].reshape(256, 2048), preferred_element_type=F32)

    ACC[...] = out_part(ATS[0], 0)

    def out_step(t, carry):
        d = lax.rem(2 + 4 * t, 7) + jnp.where(lax.rem(2 + 4 * t, 7) == 0, 7, 0)
        remote(ATR.at[d], ATR.at[d], at_s.at[d], at_r.at[d], sibling).wait_recv()
        ACC[...] += out_part(ATR[d], d)
        return carry

    lax.fori_loop(0, 7, out_step, 0)
    out[...] = ACC[...].astype(BF)

    for k in range(1, 8):
        idc[k].wait_send()
        remote(ATS.at[k], ATR.at[k], at_s.at[k], at_r.at[k], sibling).wait_send()
    for name in plan:
        if name not in ("F1", "G1", "D", "E", "H", "I"):
            send[name].wait_send()
    for i in range(3):
        for dx in (1, 3, 2):
            w_piece(dx, 4 + i, 1 + i).wait_send()
    w_own.wait_send()
    w_swap.wait_send()
    for b in range(8):
        sib_copy(b).wait_send()
        off_copy(b).wait_send()
        w_sib(b, 0).wait_send()
        w_sib(b, 1).wait_send()
    for k in range(7):
        dx, f = ((0, 0), (0, 1), (-1, 0), (1, 0), (-1, 1), (1, 1), (2, 0))[k]
        relay_copy(mod(x + dx, NX) * 2 + lax.rem(1 - yl + f, 2)).wait_send()
    ids_sib.wait_send()
    ids_off.wait_send()
    ids_rel.wait_send()
    for (part, leaning), n in STEPS.items():
        for s in range(1, n + 1):
            w_send(s, part, leaning).wait_send()


def shards(frames, qkv_weight, out_weight, recording):
    dma = pltpu.SemaphoreType.DMA
    any_ = pl.BlockSpec(memory_space=pl.ANY)
    vmem = pl.BlockSpec(memory_space=pltpu.VMEM)
    V = pltpu.VMEM
    return pl.pallas_call(
        kernel,
        name="encoder_block",
        out_shape=jax.ShapeDtypeStruct((128, 2048), BF),
        in_specs=[any_, any_, any_, vmem],
        out_specs=vmem,
        scratch_shapes=[
            V((8, 128, 2048), BF),
            V((2048, 768), BF),
            V((8, 8, 2, 16, 2048), BF),
            V((8, 128, 256), BF),
            V((8, 2, 128, 256), BF),
            V((16, 2, 128, 256), BF),
            V((8, 2, 128, 256), BF),
            V((8, 1, 128), jnp.int32),
            V((16, 1, 128), jnp.int32),
            V((8, 1, 128), jnp.int32),
            V((8, 128, 128), jnp.int32),
            V((8, 128, 256), BF),
            V((8, 128, 256), BF),
            V((128, 2048), F32),
            V((4, 2, 256, 1), F32),
            V((4, 2, 256, 1), F32),
            V((4, 2, 256, 128), F32),
            dma((3,)),
            dma((16,)), dma((16,)),
            dma((8,)), dma((8,)),
            dma((3,)), dma((3,)),
            dma((8,)), dma((8,)),
            dma((8,)), dma((8,)),
            dma((8,)), dma((8,)),
            dma((20,)), dma((20,)),
            dma((2,)), dma((2,)),
            dma((10,)), dma((10,)),
            dma((10,)), dma((10,)),
            dma((16,)), dma((16,)),
            dma((8,)), dma((8,)),
        ],
        compiler_params=pltpu.CompilerParams(
            collective_id=0, has_side_effects=True, vmem_limit_bytes=56 * 2**20
        ),
    )(frames, qkv_weight, out_weight.reshape(8, 2, 16, 2048), recording.reshape(1, 128))


def solution(mesh):
    in_specs = (P(("blk", "head"), None), P(None, "head"), P("head", None), P(("blk", "head")))
    out_specs = P(("blk", "head"), None)
    return jax.shard_map(shards, mesh=mesh, in_specs=in_specs, out_specs=out_specs, check_vma=False)
```

```python
import functools

import jax
import jax.numpy as jnp
from jax import lax
from jax.experimental import pallas as pl
from jax.experimental.pallas import tpu as pltpu
from jax.sharding import PartitionSpec as P

HEAD_DIM = 128
MESH = pl.DeviceIdType.MESH
NX, NZ, NB = 4, 8, 32
BF = jnp.bfloat16
F32 = jnp.float32
NEG = -jnp.inf


def mod(a, n):
    return lax.rem(a + 2 * n, n)


def kernel(
    frames, qw_in, ow, ids, out,
    F, QW, W, Q, KV, H, RL, IDS, HID, RID, QID, ATS, ATR, ACC, M, L, A,
    loc, ag_s, ag_r, id_s, id_r, hid_s, hid_r, sib_s, sib_r, off_s, off_r, rel_s, rel_r,
    wp_s, wp_r, wx_s, wx_r, wu_s, wu_r, wd_s, wd_r, ws_s, ws_r, at_s, at_r,
):
    blk = lax.axis_index("blk")
    head = lax.axis_index("head")
    z = blk // 4
    yh = lax.rem(blk, 4) // 2
    c = lax.rem(blk, 2)
    x = head // 2
    yl = lax.rem(head, 2)

    def block(dx, f):
        return mod(x + dx, NX) * 2 + lax.rem(yl + f, 2)

    def peer(dx, f):
        return (blk, block(dx, f))

    right, left, across = peer(1, 0), peer(-1, 0), peer(0, 1)
    sibling = (blk + 1 - 2 * c, head)
    lean = 1 - 2 * yh
    ahead = (mod(blk + 4 * lean, NB), head)
    behind = (mod(blk - 4 * lean, NB), head)
    owner_blk = z * 4 + (1 - yh) * 2 + c
    owner_head = x * 2 + 1 - yl
    relay = (owner_blk, owner_head)
    relay_to = (mod(owner_blk + 2 * c - 1, NB), owner_head)
    far = mod(blk + 2 * c - 1, NB)
    relay_from = ((far // 4) * 4 + (1 - lax.rem(far, 4) // 2) * 2 + lax.rem(far, 2), owner_head)
    base_off = 8 * (1 - c)
    base_sib = 8 * c

    def remote(src, dst, ss, rs, dev):
        return pltpu.make_async_remote_copy(
            src_ref=src, dst_ref=dst, send_sem=ss, recv_sem=rs, device_id=dev, device_id_type=MESH
        )

    load_qw = pltpu.make_async_copy(qw_in, QW, loc.at[0])
    load_own = pltpu.make_async_copy(frames, F.at[head], loc.at[1])
    load_w = pltpu.make_async_copy(ow, W.at[0], loc.at[2])
    load_own.start()
    load_qw.start()
    load_w.start()
    rels = [(dx, f) for f in range(2) for dx in range(NX)]
    partners = [peer(dx, f) for dx, f in rels[1:]]
    partners += [sibling, ahead, behind, relay, relay_to, relay_from, (far, head)]
    barrier = pltpu.get_barrier_semaphore()
    for p in partners:
        pl.semaphore_signal(barrier, inc=1, device_id=p, device_id_type=MESH)
    pl.semaphore_wait(barrier, len(partners))

    idc = [None]
    for k in range(1, 8):
        dx, f = rels[k]
        back = f * NX + (-dx) % NX
        idc.append(remote(ids, IDS.at[head], id_s.at[k], id_r.at[back], peer(dx, f)))
        idc[k].start()
    IDS[head] = ids[...]

    def w_piece(dx, s, i):
        zs = mod(z + s * lean, NZ)
        back = (-dx) % NX
        return remote(ow.at[zs, c], W.at[back, zs, c], wp_s.at[5 * dx + i], wp_r.at[5 * back + i], peer(dx, 0))

    def w_piece_wait(dx, s, i):
        ref = W.at[dx, mod(z + s * lean, NZ), c]
        remote(ref, ref, wp_s.at[5 * dx + i], wp_r.at[5 * dx + i], right).wait_recv()

    for dx in (1, 3, 2):
        w_piece(dx, 0, 0).start()
    w_own = remote(ow.at[z, c], W.at[4, z, c], wx_s.at[1], wx_r.at[1], relay)
    w_own.start()

    def fr(dx, f, start, rows=64):
        return F.at[block(dx, f), pl.ds(start, rows)]

    def gather_copy(i, src, dst, dev):
        return remote(src, dst, ag_s.at[i], ag_r.at[i], dev)

    plan = {
        "A0": ((0, 0, 0), right, (-1, 0, 0)),
        "B1": ((0, 0, 64), left, (1, 0, 64)),
        "C0": ((0, 0, 0), across, (0, 1, 0)),
        "A1": ((0, 0, 64), right, (-1, 0, 64)),
        "B0": ((0, 0, 0), left, (1, 0, 0)),
        "C1": ((0, 0, 64), across, (0, 1, 64)),
        "F0": ((0, 1, 0), right, (-1, 1, 0)),
        "G0": ((0, 1, 32, 32), left, (1, 1, 32, 32)),
        "F1": ((0, 1, 64, 32), right, (-1, 1, 64, 32)),
        "G1": ((0, 1, 64), left, (1, 1, 64)),
        "J": ((-1, 0, 96, 32), across, (-1, 1, 96, 32)),
        "K": ((1, 0, 0, 32), across, (1, 1, 0, 32)),
        "D": ((-1, 0, 0), right, (2, 0, 0)),
        "E": ((1, 0, 64), left, (2, 0, 64)),
        "H": ((-1, 1, 0), right, (2, 1, 0)),
        "I": ((1, 1, 64), left, (2, 1, 64)),
    }
    send, recv = {}, {}
    for i, (name, (what, to, comes)) in enumerate(plan.items()):
        src = frames.at[pl.ds(what[2], 64)] if what[:2] == (0, 0) else fr(*what)
        send[name] = gather_copy(i, src, fr(*what), to)
        recv[name] = gather_copy(i, fr(*comes), fr(*comes), to)
    send["C0"].start()

    def sib_copy(b):
        return remote(KV.at[b], H.at[base_sib + b], sib_s.at[b], sib_r.at[b], sibling)

    def off_copy(b):
        return remote(KV.at[b], RL.at[b], off_s.at[b], off_r.at[b], relay)

    def direct_copy(b):
        return remote(KV.at[b], H.at[base_off + b], off_s.at[b], rel_r.at[b], (far, head))

    def relay_copy(b):
        return remote(RL.at[b], H.at[base_off + b], rel_s.at[b], rel_r.at[b], relay_to)

    def project(b, direct=False):
        r = jnp.dot(F[b], QW[...], preferred_element_type=F32).astype(BF)
        for hd in range(2):
            o = hd * 3 * HEAD_DIM
            cols = pl.ds(hd * HEAD_DIM, HEAD_DIM)
            Q[b, :, cols] = r[:, o : o + HEAD_DIM]
            KV[b, 0, :, cols] = r[:, o + HEAD_DIM : o + 2 * HEAD_DIM]
            KV[b, 1, :, cols] = r[:, o + 2 * HEAD_DIM : o + 3 * HEAD_DIM]
        (direct_copy(b) if direct else off_copy(b)).start()
        sib_copy(b).start()

    def pass_on(dx, f):
        b = mod(x + dx, NX) * 2 + lax.rem(1 - yl + f, 2)
        remote(RL.at[b], RL.at[b], off_s.at[b], off_r.at[b], relay).wait_recv()
        relay_copy(b).start()

    PART = ((1, 3), (4, 4))
    STEPS = {(0, True): 1, (0, False): 3, (1, True): 3, (1, False): 4}

    def w_set(s, part, core):
        return W.at[pl.ds(*PART[part]), mod(z + s * lean, NZ), core]

    def w_copy(ref, s, part, leaning):
        i = part * 5 + s
        if leaning:
            return remote(ref, ref, wu_s.at[i], wu_r.at[i], ahead)
        return remote(ref, ref, wd_s.at[i], wd_r.at[i], behind)

    def w_send(s, part, leaning):
        return w_copy(w_set((1 - s) if leaning else (s - 1), part, c), s, part, leaning)

    def w_recv(s, part, leaning):
        return w_copy(w_set(-s if leaning else s, part, c), s, part, leaning)

    def w_sib(j, part):
        ref = w_set(j, part, c)
        return remote(ref, ref, ws_s.at[part * 8 + j], ws_r.at[part * 8 + j], sibling)

    def w_sib_recv(j, part):
        ref = w_set(j, part, 1 - c)
        return remote(ref, ref, ws_s.at[part * 8 + j], ws_r.at[part * 8 + j], sibling)

    def w_first(part):
        w_send(1, part, True).start()
        w_send(1, part, False).start()
        w_sib(0, part).start()

    def w_step(s, part, leaning):
        w_recv(s, part, leaning).wait_recv()
        if s < STEPS[part, leaning]:
            w_send(s + 1, part, leaning).start()
        w_sib(8 - s if leaning else s, part).start()

    w_swap = remote(W.at[pl.ds(1, 3), z, c], W.at[pl.ds(5, 3), z, c], wx_s.at[0], wx_r.at[0], relay)

    load_own.wait()
    load_qw.wait()
    for dx in (1, 3, 2):
        w_piece(dx, 0, 0).wait_send()
    for name in ("A0", "B1", "A1", "B0", "C1"):
        send[name].start()
    load_w.wait()
    for dx in (1, 3, 2):
        w_piece_wait(dx, 0, 0)
    w_swap.start()
    w_first(0)
    project(head)

    scale = HEAD_DIM ** (-0.5)
    dims = (((1,), (1,)), ((), ()))

    def attend(dx, chunks, first, last):
        a = mod(x + dx, NX)
        q_at = pl.ds(2 * a, 2)
        qid = QID[q_at].reshape(256, 128)
        kid = jnp.concatenate([r[b + j] for _, r, b in chunks for j in range(2)], axis=1)
        mask = jnp.concatenate([qid] * (2 * len(chunks)), axis=1) == kid
        for hd in range(2):
            cols = pl.ds(hd * HEAD_DIM, HEAD_DIM)
            q = Q[q_at, :, cols].reshape(256, HEAD_DIM)
            k, v = (
                jnp.concatenate([r[pl.ds(b, 2), n, :, cols].reshape(256, HEAD_DIM) for r, _, b in chunks], axis=0)
                for n in range(2)
            )
            s = lax.dot_general(q, k, dims, preferred_element_type=F32) * scale
            s = jnp.where(mask, s, NEG)
            m = jnp.max(s, axis=1, keepdims=True)
            if not first:
                m0 = M[a, hd]
                m = jnp.maximum(m0, m)
                decay = jnp.exp(m0 - m)
            p = jnp.exp(s - m)
            total = jnp.sum(p, axis=1, keepdims=True)
            mixed = jnp.dot(p.astype(BF), v, preferred_element_type=F32)
            if not first:
                total = L[a, hd] * decay + total
                mixed = A[a, hd] * decay + mixed
            if last:
                mixed = (mixed / total).astype(BF)
                for f in range(2):
                    rel = lax.rem(yl + f, 2) * NX + dx
                    ATS[rel, :, cols] = mixed[128 * f : 128 * (f + 1)]
            else:
                M[a, hd] = m
                L[a, hd] = total
                A[a, hd] = mixed

    def own(dx):
        return (KV, IDS, 2 * mod(x + dx, NX))

    def halo(dx, side):
        return (H, HID, 8 * side + 2 * mod(x + dx, NX))

    def facing(dx, key_dx):
        side = jnp.where(mod(x + key_dx, NX) >= mod(x + dx, NX), 0, 1)
        return halo(key_dx, side)

    near = (0, 1, -1)

    def each_near(body, then=()):
        def step(t, carry):
            body(lax.rem(3 + t, NX))
            for n, event in enumerate(then):
                pl.when(t == n)(event)
            return carry

        lax.fori_loop(0, 3, step, 0)

    def halo_wait(dx, f):
        b = block(dx, f)
        hs, ho = H.at[8 - base_sib + b], H.at[8 - base_off + b]
        remote(hs, hs, sib_s.at[b], sib_r.at[b], sibling).wait_recv()
        remote(ho, ho, rel_s.at[b], rel_r.at[b], sibling).wait_recv()

    def near_halo_wait(dx):
        if dx == 0:
            hs, ho = HID.at[pl.ds(8 - base_sib, 8)], HID.at[pl.ds(8 - base_off, 8)]
            remote(hs, hs, hid_s.at[0], hid_r.at[0], sibling).wait_recv()
            remote(ho, ho, hid_s.at[2], hid_r.at[2], sibling).wait_recv()
        halo_wait(dx, 0)
        halo_wait(dx, 1)

    w_step(1, 0, False)
    w_step(1, 0, True)
    w_own.wait_recv()
    w_swap.wait_recv()
    w_first(1)
    recv["C0"].wait_recv()
    send["F0"].start()
    send["G0"].start()
    recv["C1"].wait_recv()
    send["F1"].start()
    send["G1"].start()
    pass_on(0, 0)
    for k in range(1, 8):
        dx, f = rels[k]
        row = IDS.at[block(dx, f)]
        remote(row, row, id_s.at[k], id_r.at[k], across).wait_recv()
    ids_sib = remote(IDS, HID.at[pl.ds(base_sib, 8)], hid_s.at[0], hid_r.at[0], sibling)
    ids_off = remote(IDS, RID, hid_s.at[1], hid_r.at[1], relay)
    ids_rel = remote(RID, HID.at[pl.ds(base_off, 8)], hid_s.at[2], hid_r.at[2], relay_to)
    ids_off.start()
    ids_sib.start()
    for b in range(8):
        QID[b] = jnp.transpose(jnp.broadcast_to(IDS[b], (128, 128)))
    project(block(0, 1))
    recv["A0"].wait_recv()
    recv["A1"].wait_recv()
    send["J"].start()
    recv["B1"].wait_recv()
    recv["B0"].wait_recv()
    send["K"].start()
    project(block(-1, 0))
    project(block(1, 0))
    w_step(1, 1, True)
    w_step(2, 0, False)
    w_step(1, 1, False)
    pass_on(0, 1)
    ids_off.wait_recv()
    ids_rel.start()
    send["F1"].wait_send()
    send["D"].start()
    send["G1"].wait_send()
    send["E"].start()
    recv["F0"].wait_recv()
    send["H"].start()
    recv["G1"].wait_recv()
    send["I"].start()
    recv["G0"].wait_recv()
    recv["K"].wait_recv()
    project(block(1, 1))
    recv["F1"].wait_recv()
    recv["J"].wait_recv()
    project(block(-1, 1))
    pass_on(-1, 0)
    pass_on(1, 0)
    w_step(2, 1, True)
    near_halo_wait(0)
    def between_0():
        w_step(2, 1, False)

    def between_1():
        w_step(3, 0, False)
        pass_on(1, 1)

    each_near(
        lambda dx: attend(dx, [own(n) for n in near] + [facing(dx, 0)], True, False), (between_0, between_1)
    )
    pass_on(-1, 1)
    for name in ("D", "E", "H", "I"):
        send[name].wait_send()
    for i in range(3):
        for dx in (1, 3, 2):
            w_piece(dx, 4 + i, 1 + i).start()
    recv["D"].wait_recv()
    recv["E"].wait_recv()
    project(block(2, 0))
    recv["H"].wait_recv()
    recv["I"].wait_recv()
    project(block(2, 1), direct=True)
    attend(2, [own(n) for n in near] + [own(2)], True, False)
    pass_on(2, 0)
    w_step(3, 1, False)
    near_halo_wait(1)
    near_halo_wait(-1)
    each_near(lambda dx: attend(dx, [own(2), facing(dx, 1), facing(dx, -1), halo(dx, 1)], False, False))
    w_step(3, 1, True)
    attend(2, [facing(2, n) for n in near], False, False)
    w_step(4, 1, False)
    for i in range(3):
        for dx in (1, 3, 2):
            w_piece_wait(dx, 4 + i, 1 + i)
        w_sib(4 + i, 0).start()
    halo_wait(2, 0)
    halo_wait(2, 1)

    def hand_over(dx):
        for f in range(2):
            rel = f * NX + dx
            back = f * NX + mod(-dx, NX)

            @pl.when(rel > 0)
            def _():
                remote(ATS.at[rel], ATR.at[back], at_s.at[rel], at_r.at[back], peer(dx, f)).start()

    def finish(dx, chunks):
        attend(dx, chunks, False, True)
        hand_over(dx)

    finish(2, [halo(2, 0), halo(2, 1)])
    each_near(lambda dx: finish(dx, [facing(dx, 2)]))

    for j in range(8):
        w_sib_recv(j, 0).wait_recv()
        w_sib_recv(j, 1).wait_recv()

    def out_part(a, d):
        return jnp.dot(a, W[d].reshape(256, 2048), preferred_element_type=F32)

    ACC[...] = out_part(ATS[0], 0)

    def out_step(t, carry):
        d = lax.rem(2 + 4 * t, 7) + jnp.where(lax.rem(2 + 4 * t, 7) == 0, 7, 0)
        remote(ATR.at[d], ATR.at[d], at_s.at[d], at_r.at[d], sibling).wait_recv()
        ACC[...] += out_part(ATR[d], d)
        return carry

    lax.fori_loop(0, 7, out_step, 0)
    out[...] = ACC[...].astype(BF)

    for k in range(1, 8):
        idc[k].wait_send()
        remote(ATS.at[k], ATR.at[k], at_s.at[k], at_r.at[k], sibling).wait_send()
    for name in plan:
        if name not in ("F1", "G1", "D", "E", "H", "I"):
            send[name].wait_send()
    for i in range(3):
        for dx in (1, 3, 2):
            w_piece(dx, 4 + i, 1 + i).wait_send()
    w_own.wait_send()
    w_swap.wait_send()
    for b in range(8):
        sib_copy(b).wait_send()
        off_copy(b).wait_send()
        w_sib(b, 0).wait_send()
        w_sib(b, 1).wait_send()
    for k in range(7):
        dx, f = ((0, 0), (0, 1), (-1, 0), (1, 0), (-1, 1), (1, 1), (2, 0))[k]
        relay_copy(mod(x + dx, NX) * 2 + lax.rem(1 - yl + f, 2)).wait_send()
    ids_sib.wait_send()
    ids_off.wait_send()
    ids_rel.wait_send()
    for (part, leaning), n in STEPS.items():
        for s in range(1, n + 1):
            w_send(s, part, leaning).wait_send()


def shards(frames, qkv_weight, out_weight, recording):
    dma = pltpu.SemaphoreType.DMA
    any_ = pl.BlockSpec(memory_space=pl.ANY)
    vmem = pl.BlockSpec(memory_space=pltpu.VMEM)
    V = pltpu.VMEM
    return pl.pallas_call(
        kernel,
        name="encoder_block",
        out_shape=jax.ShapeDtypeStruct((128, 2048), BF),
        in_specs=[any_, any_, any_, vmem],
        out_specs=vmem,
        scratch_shapes=[
            V((8, 128, 2048), BF),
            V((2048, 768), BF),
            V((8, 8, 2, 16, 2048), BF),
            V((8, 128, 256), BF),
            V((8, 2, 128, 256), BF),
            V((16, 2, 128, 256), BF),
            V((8, 2, 128, 256), BF),
            V((8, 1, 128), jnp.int32),
            V((16, 1, 128), jnp.int32),
            V((8, 1, 128), jnp.int32),
            V((8, 128, 128), jnp.int32),
            V((8, 128, 256), BF),
            V((8, 128, 256), BF),
            V((128, 2048), F32),
            V((4, 2, 256, 1), F32),
            V((4, 2, 256, 1), F32),
            V((4, 2, 256, 128), F32),
            dma((3,)),
            dma((16,)), dma((16,)),
            dma((8,)), dma((8,)),
            dma((3,)), dma((3,)),
            dma((8,)), dma((8,)),
            dma((8,)), dma((8,)),
            dma((8,)), dma((8,)),
            dma((20,)), dma((20,)),
            dma((2,)), dma((2,)),
            dma((10,)), dma((10,)),
            dma((10,)), dma((10,)),
            dma((16,)), dma((16,)),
            dma((8,)), dma((8,)),
        ],
        compiler_params=pltpu.CompilerParams(
            collective_id=0, has_side_effects=True, vmem_limit_bytes=56 * 2**20
        ),
    )(frames, qkv_weight, out_weight.reshape(8, 2, 16, 2048), recording.reshape(1, 128))


def solution(mesh):
    in_specs = (P(("blk", "head"), None), P(None, "head"), P("head", None), P(("blk", "head")))
    out_specs = P(("blk", "head"), None)
    return jax.shard_map(shards, mesh=mesh, in_specs=in_specs, out_specs=out_specs, check_vma=False)
```

```python
import functools

import jax
import jax.numpy as jnp
from jax import lax
from jax.experimental import pallas as pl
from jax.experimental.pallas import tpu as pltpu
from jax.sharding import PartitionSpec as P

HEAD_DIM = 128
MESH = pl.DeviceIdType.MESH
NX, NZ, NB = 4, 8, 32
BF = jnp.bfloat16
F32 = jnp.float32
NEG = -jnp.inf


def mod(a, n):
    return lax.rem(a + 2 * n, n)


def kernel(
    frames, qw_in, ow, ids, out,
    F, QW, W, Q, KV, H, RL, IDS, HID, RID, QID, ATS, ATR, ACC, M, L, A,
    loc, ag_s, ag_r, id_s, id_r, hid_s, hid_r, sib_s, sib_r, off_s, off_r, rel_s, rel_r,
    wp_s, wp_r, wx_s, wx_r, wu_s, wu_r, wd_s, wd_r, ws_s, ws_r, at_s, at_r,
):
    blk = lax.axis_index("blk")
    head = lax.axis_index("head")
    z = blk // 4
    yh = lax.rem(blk, 4) // 2
    c = lax.rem(blk, 2)
    x = head // 2
    yl = lax.rem(head, 2)

    def block(dx, f):
        return mod(x + dx, NX) * 2 + lax.rem(yl + f, 2)

    def peer(dx, f):
        return (blk, block(dx, f))

    right, left, across = peer(1, 0), peer(-1, 0), peer(0, 1)
    sibling = (blk + 1 - 2 * c, head)
    lean = 1 - 2 * yh
    ahead = (mod(blk + 4 * lean, NB), head)
    behind = (mod(blk - 4 * lean, NB), head)
    owner_blk = z * 4 + (1 - yh) * 2 + c
    owner_head = x * 2 + 1 - yl
    relay = (owner_blk, owner_head)
    relay_to = (mod(owner_blk + 2 * c - 1, NB), owner_head)
    far = mod(blk + 2 * c - 1, NB)
    relay_from = ((far // 4) * 4 + (1 - lax.rem(far, 4) // 2) * 2 + lax.rem(far, 2), owner_head)
    base_off = 8 * (1 - c)
    base_sib = 8 * c

    def remote(src, dst, ss, rs, dev):
        return pltpu.make_async_remote_copy(
            src_ref=src, dst_ref=dst, send_sem=ss, recv_sem=rs, device_id=dev, device_id_type=MESH
        )

    load_qw = pltpu.make_async_copy(qw_in, QW, loc.at[0])
    load_own = pltpu.make_async_copy(frames, F.at[head], loc.at[1])
    load_w = pltpu.make_async_copy(ow, W.at[0], loc.at[2])
    load_own.start()
    load_qw.start()
    load_w.start()
    rels = [(dx, f) for f in range(2) for dx in range(NX)]
    partners = [peer(dx, f) for dx, f in rels[1:]]
    partners += [sibling, ahead, behind, relay, relay_to, relay_from, (far, head)]
    barrier = pltpu.get_barrier_semaphore()
    for p in partners:
        pl.semaphore_signal(barrier, inc=1, device_id=p, device_id_type=MESH)
    pl.semaphore_wait(barrier, len(partners))

    idc = [None]
    for k in range(1, 8):
        dx, f = rels[k]
        back = f * NX + (-dx) % NX
        idc.append(remote(ids, IDS.at[head], id_s.at[k], id_r.at[back], peer(dx, f)))
        idc[k].start()
    IDS[head] = ids[...]

    def w_piece(dx, s, i):
        zs = mod(z + s * lean, NZ)
        back = (-dx) % NX
        return remote(ow.at[zs, c], W.at[back, zs, c], wp_s.at[5 * dx + i], wp_r.at[5 * back + i], peer(dx, 0))

    def w_piece_wait(dx, s, i):
        ref = W.at[dx, mod(z + s * lean, NZ), c]
        remote(ref, ref, wp_s.at[5 * dx + i], wp_r.at[5 * dx + i], right).wait_recv()

    for dx in (1, 3, 2):
        w_piece(dx, 0, 0).start()
    w_own = remote(ow.at[z, c], W.at[4, z, c], wx_s.at[1], wx_r.at[1], relay)
    w_own.start()

    def fr(dx, f, start, rows=64):
        return F.at[block(dx, f), pl.ds(start, rows)]

    def gather_copy(i, src, dst, dev):
        return remote(src, dst, ag_s.at[i], ag_r.at[i], dev)

    plan = {
        "A0": ((0, 0, 0), right, (-1, 0, 0)),
        "B1": ((0, 0, 64), left, (1, 0, 64)),
        "C0": ((0, 0, 0), across, (0, 1, 0)),
        "A1": ((0, 0, 64), right, (-1, 0, 64)),
        "B0": ((0, 0, 0), left, (1, 0, 0)),
        "C1": ((0, 0, 64), across, (0, 1, 64)),
        "F0": ((0, 1, 0), right, (-1, 1, 0)),
        "G0": ((0, 1, 32, 32), left, (1, 1, 32, 32)),
        "F1": ((0, 1, 64, 32), right, (-1, 1, 64, 32)),
        "G1": ((0, 1, 64), left, (1, 1, 64)),
        "J": ((-1, 0, 96, 32), across, (-1, 1, 96, 32)),
        "K": ((1, 0, 0, 32), across, (1, 1, 0, 32)),
        "D": ((-1, 0, 0), right, (2, 0, 0)),
        "E": ((1, 0, 64), left, (2, 0, 64)),
        "H": ((-1, 1, 0), right, (2, 1, 0)),
        "I": ((1, 1, 64), left, (2, 1, 64)),
    }
    send, recv = {}, {}
    for i, (name, (what, to, comes)) in enumerate(plan.items()):
        src = frames.at[pl.ds(what[2], 64)] if what[:2] == (0, 0) else fr(*what)
        send[name] = gather_copy(i, src, fr(*what), to)
        recv[name] = gather_copy(i, fr(*comes), fr(*comes), to)
    send["C0"].start()

    def sib_copy(b):
        return remote(KV.at[b], H.at[base_sib + b], sib_s.at[b], sib_r.at[b], sibling)

    def off_copy(b):
        return remote(KV.at[b], RL.at[b], off_s.at[b], off_r.at[b], relay)

    def direct_copy(b):
        return remote(KV.at[b], H.at[base_off + b], off_s.at[b], rel_r.at[b], (far, head))

    def relay_copy(b):
        return remote(RL.at[b], H.at[base_off + b], rel_s.at[b], rel_r.at[b], relay_to)

    def project(b, direct=False):
        r = jnp.dot(F[b], QW[...], preferred_element_type=F32).astype(BF)
        for hd in range(2):
            o = hd * 3 * HEAD_DIM
            cols = pl.ds(hd * HEAD_DIM, HEAD_DIM)
            Q[b, :, cols] = r[:, o : o + HEAD_DIM]
            KV[b, 0, :, cols] = r[:, o + HEAD_DIM : o + 2 * HEAD_DIM]
            KV[b, 1, :, cols] = r[:, o + 2 * HEAD_DIM : o + 3 * HEAD_DIM]
        (direct_copy(b) if direct else off_copy(b)).start()
        sib_copy(b).start()

    def pass_on(dx, f):
        b = mod(x + dx, NX) * 2 + lax.rem(1 - yl + f, 2)
        remote(RL.at[b], RL.at[b], off_s.at[b], off_r.at[b], relay).wait_recv()
        relay_copy(b).start()

    PART = ((1, 3), (4, 4))
    STEPS = {(0, True): 1, (0, False): 3, (1, True): 3, (1, False): 4}

    def w_set(s, part, core):
        return W.at[pl.ds(*PART[part]), mod(z + s * lean, NZ), core]

    def w_copy(ref, s, part, leaning):
        i = part * 5 + s
        if leaning:
            return remote(ref, ref, wu_s.at[i], wu_r.at[i], ahead)
        return remote(ref, ref, wd_s.at[i], wd_r.at[i], behind)

    def w_send(s, part, leaning):
        return w_copy(w_set((1 - s) if leaning else (s - 1), part, c), s, part, leaning)

    def w_recv(s, part, leaning):
        return w_copy(w_set(-s if leaning else s, part, c), s, part, leaning)

    def w_sib(j, part):
        ref = w_set(j, part, c)
        return remote(ref, ref, ws_s.at[part * 8 + j], ws_r.at[part * 8 + j], sibling)

    def w_sib_recv(j, part):
        ref = w_set(j, part, 1 - c)
        return remote(ref, ref, ws_s.at[part * 8 + j], ws_r.at[part * 8 + j], sibling)

    def w_first(part):
        w_send(1, part, True).start()
        w_send(1, part, False).start()
        w_sib(0, part).start()

    def w_step(s, part, leaning):
        w_recv(s, part, leaning).wait_recv()
        if s < STEPS[part, leaning]:
            w_send(s + 1, part, leaning).start()
        w_sib(8 - s if leaning else s, part).start()

    w_swap = remote(W.at[pl.ds(1, 3), z, c], W.at[pl.ds(5, 3), z, c], wx_s.at[0], wx_r.at[0], relay)

    load_own.wait()
    load_qw.wait()
    for dx in (1, 3, 2):
        w_piece(dx, 0, 0).wait_send()
    for name in ("A0", "B1", "A1", "B0", "C1"):
        send[name].start()
    load_w.wait()
    for dx in (1, 3, 2):
        w_piece_wait(dx, 0, 0)
    w_swap.start()
    w_first(0)
    project(head)

    scale = HEAD_DIM ** (-0.5)
    dims = (((1,), (1,)), ((), ()))

    def attend(dx, chunks, first, last):
        a = mod(x + dx, NX)
        q_at = pl.ds(2 * a, 2)
        qid = QID[q_at].reshape(256, 128)
        kid = jnp.concatenate([r[b + j] for _, r, b in chunks for j in range(2)], axis=1)
        mask = jnp.concatenate([qid] * (2 * len(chunks)), axis=1) == kid
        for hd in range(2):
            cols = pl.ds(hd * HEAD_DIM, HEAD_DIM)
            q = Q[q_at, :, cols].reshape(256, HEAD_DIM)
            k, v = (
                jnp.concatenate([r[pl.ds(b, 2), n, :, cols].reshape(256, HEAD_DIM) for r, _, b in chunks], axis=0)
                for n in range(2)
            )
            s = lax.dot_general(q, k, dims, preferred_element_type=F32) * scale
            s = jnp.where(mask, s, NEG)
            m = jnp.max(s, axis=1, keepdims=True)
            if not first:
                m0 = M[a, hd]
                m = jnp.maximum(m0, m)
                decay = jnp.exp(m0 - m)
            p = jnp.exp(s - m)
            total = jnp.sum(p, axis=1, keepdims=True)
            mixed = jnp.dot(p.astype(BF), v, preferred_element_type=F32)
            if not first:
                total = L[a, hd] * decay + total
                mixed = A[a, hd] * decay + mixed
            if last:
                mixed = (mixed / total).astype(BF)
                for f in range(2):
                    rel = lax.rem(yl + f, 2) * NX + dx
                    ATS[rel, :, cols] = mixed[128 * f : 128 * (f + 1)]
            else:
                M[a, hd] = m
                L[a, hd] = total
                A[a, hd] = mixed

    def own(dx):
        return (KV, IDS, 2 * mod(x + dx, NX))

    def halo(dx, side):
        return (H, HID, 8 * side + 2 * mod(x + dx, NX))

    def facing(dx, key_dx):
        side = jnp.where(mod(x + key_dx, NX) >= mod(x + dx, NX), 0, 1)
        return halo(key_dx, side)

    near = (0, 1, -1)

    def each_near(body, then=()):
        def step(t, carry):
            body(lax.rem(3 + t, NX))
            for n, event in enumerate(then):
                pl.when(t == n)(event)
            return carry

        lax.fori_loop(0, 3, step, 0)

    def halo_wait(dx, f):
        b = block(dx, f)
        hs, ho = H.at[8 - base_sib + b], H.at[8 - base_off + b]
        remote(hs, hs, sib_s.at[b], sib_r.at[b], sibling).wait_recv()
        remote(ho, ho, rel_s.at[b], rel_r.at[b], sibling).wait_recv()

    def near_halo_wait(dx):
        if dx == 0:
            hs, ho = HID.at[pl.ds(8 - base_sib, 8)], HID.at[pl.ds(8 - base_off, 8)]
            remote(hs, hs, hid_s.at[0], hid_r.at[0], sibling).wait_recv()
            remote(ho, ho, hid_s.at[2], hid_r.at[2], sibling).wait_recv()
        halo_wait(dx, 0)
        halo_wait(dx, 1)

    w_step(1, 0, False)
    w_step(1, 0, True)
    w_own.wait_recv()
    w_swap.wait_recv()
    w_first(1)
    recv["C0"].wait_recv()
    send["F0"].start()
    send["G0"].start()
    recv["C1"].wait_recv()
    send["F1"].start()
    send["G1"].start()
    pass_on(0, 0)
    for k in range(1, 8):
        dx, f = rels[k]
        row = IDS.at[block(dx, f)]
        remote(row, row, id_s.at[k], id_r.at[k], across).wait_recv()
    ids_sib = remote(IDS, HID.at[pl.ds(base_sib, 8)], hid_s.at[0], hid_r.at[0], sibling)
    ids_off = remote(IDS, RID, hid_s.at[1], hid_r.at[1], relay)
    ids_rel = remote(RID, HID.at[pl.ds(base_off, 8)], hid_s.at[2], hid_r.at[2], relay_to)
    ids_off.start()
    ids_sib.start()
    for b in range(8):
        QID[b] = jnp.transpose(jnp.broadcast_to(IDS[b], (128, 128)))
    project(block(0, 1))
    recv["A0"].wait_recv()
    recv["A1"].wait_recv()
    send["J"].start()
    recv["B1"].wait_recv()
    recv["B0"].wait_recv()
    send["K"].start()
    lax.fori_loop(0, 2, lambda t, carry: (project(block(3 - 2 * t, 0)), carry)[1], 0)
    w_step(1, 1, True)
    w_step(2, 0, False)
    w_step(1, 1, False)
    pass_on(0, 1)
    ids_off.wait_recv()
    ids_rel.start()
    send["F1"].wait_send()
    send["D"].start()
    send["G1"].wait_send()
    send["E"].start()
    recv["F0"].wait_recv()
    send["H"].start()
    recv["G1"].wait_recv()
    send["I"].start()
    recv["G0"].wait_recv()
    recv["K"].wait_recv()
    project(block(1, 1))
    recv["F1"].wait_recv()
    recv["J"].wait_recv()
    project(block(-1, 1))
    pass_on(-1, 0)
    pass_on(1, 0)
    w_step(2, 1, True)
    near_halo_wait(0)
    def between_0():
        w_step(2, 1, False)

    def between_1():
        w_step(3, 0, False)
        pass_on(1, 1)

    each_near(
        lambda dx: attend(dx, [own(n) for n in near] + [facing(dx, 0)], True, False), (between_0, between_1)
    )
    pass_on(-1, 1)
    for name in ("D", "E", "H", "I"):
        send[name].wait_send()
    for i in range(3):
        for dx in (1, 3, 2):
            w_piece(dx, 4 + i, 1 + i).start()
    recv["D"].wait_recv()
    recv["E"].wait_recv()
    project(block(2, 0))
    recv["H"].wait_recv()
    recv["I"].wait_recv()
    project(block(2, 1), direct=True)
    attend(2, [own(n) for n in near] + [own(2)], True, False)
    pass_on(2, 0)
    w_step(3, 1, False)
    near_halo_wait(1)
    near_halo_wait(-1)
    each_near(lambda dx: attend(dx, [own(2), facing(dx, 1), facing(dx, -1), halo(dx, 1)], False, False))
    w_step(3, 1, True)
    attend(2, [facing(2, n) for n in near], False, False)
    w_step(4, 1, False)
    for i in range(3):
        for dx in (1, 3, 2):
            w_piece_wait(dx, 4 + i, 1 + i)
        w_sib(4 + i, 0).start()
    halo_wait(2, 0)
    halo_wait(2, 1)

    def hand_over(dx):
        for f in range(2):
            rel = f * NX + dx
            back = f * NX + mod(-dx, NX)

            @pl.when(rel > 0)
            def _():
                remote(ATS.at[rel], ATR.at[back], at_s.at[rel], at_r.at[back], peer(dx, f)).start()

    def finish(dx, chunks):
        attend(dx, chunks, False, True)
        hand_over(dx)

    finish(2, [halo(2, 0), halo(2, 1)])
    each_near(lambda dx: finish(dx, [facing(dx, 2)]))

    for j in range(8):
        w_sib_recv(j, 0).wait_recv()
        w_sib_recv(j, 1).wait_recv()

    def out_part(a, d):
        return jnp.dot(a, W[d].reshape(256, 2048), preferred_element_type=F32)

    ACC[...] = jnp.zeros_like(ACC)
    ATR[0] = ATS[0]

    def out_step(t, carry):
        turn = lax.rem(4 * t + 5, 7)
        d = jnp.where(t == 0, 0, jnp.where(turn == 0, 7, turn))

        @pl.when(t > 0)
        def _():
            remote(ATR.at[d], ATR.at[d], at_s.at[d], at_r.at[d], sibling).wait_recv()

        ACC[...] += out_part(ATR[d], d)
        return carry

    lax.fori_loop(0, 8, out_step, 0)
    out[...] = ACC[...].astype(BF)

    for k in range(1, 8):
        idc[k].wait_send()
        remote(ATS.at[k], ATR.at[k], at_s.at[k], at_r.at[k], sibling).wait_send()
    for name in plan:
        if name not in ("F1", "G1", "D", "E", "H", "I"):
            send[name].wait_send()
    for i in range(3):
        for dx in (1, 3, 2):
            w_piece(dx, 4 + i, 1 + i).wait_send()
    w_own.wait_send()
    w_swap.wait_send()
    for b in range(8):
        sib_copy(b).wait_send()
        off_copy(b).wait_send()
        w_sib(b, 0).wait_send()
        w_sib(b, 1).wait_send()
    for k in range(7):
        dx, f = ((0, 0), (0, 1), (-1, 0), (1, 0), (-1, 1), (1, 1), (2, 0))[k]
        relay_copy(mod(x + dx, NX) * 2 + lax.rem(1 - yl + f, 2)).wait_send()
    ids_sib.wait_send()
    ids_off.wait_send()
    ids_rel.wait_send()
    for (part, leaning), n in STEPS.items():
        for s in range(1, n + 1):
            w_send(s, part, leaning).wait_send()


def shards(frames, qkv_weight, out_weight, recording):
    dma = pltpu.SemaphoreType.DMA
    any_ = pl.BlockSpec(memory_space=pl.ANY)
    vmem = pl.BlockSpec(memory_space=pltpu.VMEM)
    V = pltpu.VMEM
    return pl.pallas_call(
        kernel,
        name="encoder_block",
        out_shape=jax.ShapeDtypeStruct((128, 2048), BF),
        in_specs=[any_, any_, any_, vmem],
        out_specs=vmem,
        scratch_shapes=[
            V((8, 128, 2048), BF),
            V((2048, 768), BF),
            V((8, 8, 2, 16, 2048), BF),
            V((8, 128, 256), BF),
            V((8, 2, 128, 256), BF),
            V((16, 2, 128, 256), BF),
            V((8, 2, 128, 256), BF),
            V((8, 1, 128), jnp.int32),
            V((16, 1, 128), jnp.int32),
            V((8, 1, 128), jnp.int32),
            V((8, 128, 128), jnp.int32),
            V((8, 128, 256), BF),
            V((8, 128, 256), BF),
            V((128, 2048), F32),
            V((4, 2, 256, 1), F32),
            V((4, 2, 256, 1), F32),
            V((4, 2, 256, 128), F32),
            dma((3,)),
            dma((16,)), dma((16,)),
            dma((8,)), dma((8,)),
            dma((3,)), dma((3,)),
            dma((8,)), dma((8,)),
            dma((8,)), dma((8,)),
            dma((8,)), dma((8,)),
            dma((20,)), dma((20,)),
            dma((2,)), dma((2,)),
            dma((10,)), dma((10,)),
            dma((10,)), dma((10,)),
            dma((16,)), dma((16,)),
            dma((8,)), dma((8,)),
        ],
        compiler_params=pltpu.CompilerParams(
            collective_id=0, has_side_effects=True, vmem_limit_bytes=56 * 2**20
        ),
    )(frames, qkv_weight, out_weight.reshape(8, 2, 16, 2048), recording.reshape(1, 128))


def solution(mesh):
    in_specs = (P(("blk", "head"), None), P(None, "head"), P("head", None), P(("blk", "head")))
    out_specs = P(("blk", "head"), None)
    return jax.shard_map(shards, mesh=mesh, in_specs=in_specs, out_specs=out_specs, check_vma=False)
```
